128 devices in a mesh: genome: 32 (over y, x, core), cell: 4 (over z).
Axes of the slice: x: 4, y: 4, z: 4, core: 2. Of those that a mesh axis runs over, the one named last changes fastest.
Arguments:
- inputs: bfloat16 [4, 65536, 512], P('cell', 'genome'), may hold values from -6 to 6
- weight: bfloat16 [512, 512], replicated, may hold values from -0.25 to 0.25
- band_vals: bfloat16 [4, 512, 9, 128, 128], P('cell', 'genome'), may hold values from -1 to 1, as said below
- far_rows: int32 [4, 32, 32, 2], P('cell', 'genome'), may hold values from 0 to 15
- far_send: int32 [4, 32, 32, 2], P('cell', 'genome'), may hold values from 0 to 15
- far_count: int32 [4, 32, 32], P('cell', 'genome'), may hold values from 0 to 2, as said below
- far_vals: bfloat16 [4, 32, 32, 2, 128, 128], P('cell', 'genome'), may hold values from -0.25 to 0.25
- grad_out: bfloat16 [4, 65536, 512], P('cell', 'genome'), may hold values from -6 to 6
Outputs:
- output: bfloat16 [4, 65536, 512], P('cell', 'genome')
- grad_in: bfloat16 [4, 65536, 512], P('cell', 'genome')
- grad_weight: float32 [512, 512], replicated
The draws below stay inside these ranges and needn't reach their ends.
Inputs may be any that keep to these rules, and one draw needn't show every extreme that they name: The band is symmetric: band_vals[c, i, d] is the transpose of band_vals[c, i + d - 4, 8 - d] wherever both blocks lie in the grid. `far_count`: slots used from one sender to one receiver; for each cell type some receiving device gets 2 from every sender.
All inputs are finite; a program needn't handle non-finite values.
Results may differ from the reference program's by a relative error of at most 0.007.
Values may be sent and summed in bfloat16 or wider, within the bound.
No kernel may reach another device: no remote copies, remote signals or barrier semaphores. Data moves between devices by JAX's collectives and lax.ppermute only.
A program may use at most 192 MiB of HBM per device.

```python
import math
import jax
import jax.numpy as jnp

F = 512
BLK = 128
BAND = 4
CAP = 2
NBLK_DEV = 16
PEERS = 32
NBLKS = 512
BINS = 65536
CELLS = 4


def draw_band_vals(key, part):
    key = jax.random.fold_in(key, 11)
    shape = (CELLS, NBLKS, 2 * BAND + 1, BLK, BLK)
    raw = jnp.clip(0.4 * jax.random.normal(key, shape, jnp.float32), -1.0, 1.0)
    pieces = []
    for offset in range(2 * BAND + 1):
        mirror = jnp.roll(raw[:, :, 2 * BAND - offset], BAND - offset, axis=1)
        pieces.append(0.5 * (raw[:, :, offset] + jnp.swapaxes(mirror, -1, -2)))
    return jnp.stack(pieces, axis=2).astype(jnp.bfloat16)


def draw_far_count(key, part):
    key = jax.random.fold_in(key, 23)
    key_counts, key_hot = jax.random.split(key)
    counts = jax.random.randint(key_counts, (CELLS, PEERS, PEERS), 0, CAP + 1)
    hot_dest = jax.random.randint(key_hot, (CELLS, 1, 1), 0, PEERS)
    column = jnp.arange(PEERS, dtype=jnp.int32)[None, None, :]
    return jnp.where(column == hot_dest, CAP, counts).astype(jnp.int32)


def place_ends(values, own_key, smallest, largest):
    longest = values.shape.index(max(values.shape))
    spots = []
    for shift in (0, 1):
        where = [jax.random.randint(jax.random.fold_in(own_key, axis), (), 0, length) for axis, length in enumerate(values.shape)]
        where[longest] = (where[longest] + shift) % values.shape[longest]
        spots.append(tuple(where))
    return values.at[spots[0]].set(smallest).at[spots[1]].set(largest)


def block_levels(stream_key, extent, cuts, least, top_value):
    factor_of = 1.0
    for dim, parts in cuts:
        steps = jax.random.uniform(jax.random.fold_in(jax.random.fold_in(stream_key, 6), dim), (parts,), jnp.float32, least / len(cuts), top_value / len(cuts))
        factor_of = factor_of * jnp.repeat(jnp.exp(steps), extent[dim] // parts).reshape((-1,) + (1,) * (len(extent) - 1 - dim))
    return factor_of


def bell_draw(rng, extent, spread, most, shards=(), held_as=jnp.bfloat16):
    result = spread * jax.random.normal(rng, extent, jnp.float32)
    if shards:
        result = result * block_levels(rng, extent, shards, -0.22, 0.18)
    return jnp.clip(result, -most, most).astype(held_as)


def setup_inputs(seed: int = 0) -> dict:
    keys = jax.random.split(jax.random.key(seed), 9)
    return {
        "inputs": bell_draw(keys[0], (CELLS, BINS, F), 1.0, 6.0, ((0, 4), (1, 32))),
        "weight": bell_draw(keys[1], (F, F), F ** -0.5, 0.25),
        "band_vals": draw_band_vals(jax.random.fold_in(keys[8], 71), 0),
        "far_rows": place_ends(jax.random.randint(keys[3], (CELLS, PEERS, PEERS, CAP), 0, NBLK_DEV), jax.random.fold_in(keys[3], 1), 0, NBLK_DEV - 1).astype(jnp.int32),
        "far_send": place_ends(jax.random.randint(keys[4], (CELLS, PEERS, PEERS, CAP), 0, NBLK_DEV), jax.random.fold_in(keys[4], 1), 0, NBLK_DEV - 1).astype(jnp.int32),
        "far_count": draw_far_count(jax.random.fold_in(keys[8], 71), 0),
        "far_vals": bell_draw(keys[6], (CELLS, PEERS, PEERS, CAP, BLK, BLK), (4 * BLK) ** -0.5, 0.25, ((0, 4), (1, 32))),
        "grad_out": bell_draw(keys[7], (CELLS, BINS, F), 1.0, 6.0, ((0, 4), (1, 32))),
    }


band_gain = 3.0

def band_apply(values, band_cell):
    blocks = values.reshape(NBLKS, BLK, F).astype(jnp.float32)
    margin = jnp.zeros((BAND, BLK, F), jnp.float32)
    padded = jnp.concatenate([margin, blocks, margin], axis=0)
    summed = jnp.zeros((NBLKS, BLK, F), jnp.float32)
    for offset in range(2 * BAND + 1):
        summed = summed + jnp.einsum('nij,njf->nif', band_cell[:, offset].astype(jnp.float32), padded[offset:offset + NBLKS])
    factor = band_gain / math.sqrt((2 * BAND + 1) * BLK)
    return (factor * summed).reshape(BINS, F)

def reference(inputs, weight, band_vals, far_rows, far_send, far_count, far_vals, grad_out):
    peer_ids = jnp.arange(PEERS, dtype=jnp.int32)
    slot_ids = jnp.arange(CAP, dtype=jnp.int32)
    outputs = []
    grads_in = []
    grad_weight = jnp.zeros((F, F), jnp.float32)
    for cell in range(CELLS):
        projected = jnp.dot(inputs[cell], weight, preferred_element_type=jnp.float32).astype(jnp.bfloat16)
        source = (peer_ids[:, None, None] * NBLK_DEV + far_send[cell]).astype(jnp.int32)
        live = slot_ids[None, None, :] < far_count[cell][:, :, None]
        source_flat = jnp.transpose(source, (1, 0, 2)).reshape(-1)
        live_flat = jnp.transpose(live, (1, 0, 2)).reshape(-1)
        target_flat = (peer_ids[:, None, None] * NBLK_DEV + far_rows[cell]).astype(jnp.int32).reshape(-1)
        loop_vals = far_vals[cell].reshape(-1, BLK, BLK).astype(jnp.float32)
        zblocks = projected.reshape(NBLKS, BLK, F)
        fetched = jnp.where(live_flat[:, None, None], zblocks[source_flat], jnp.zeros((), jnp.bfloat16)).astype(jnp.float32)
        loop_terms = jnp.einsum('kij,kjf->kif', loop_vals, fetched)
        far_part = jax.ops.segment_sum(loop_terms, target_flat, num_segments=NBLKS).reshape(BINS, F)
        preact = band_apply(projected, band_vals[cell]) + far_part
        sigma = jax.nn.sigmoid(preact)
        outputs.append((preact * sigma).astype(jnp.bfloat16))
        slope = sigma * (1.0 + preact * (1.0 - sigma))
        grads = (grad_out[cell].astype(jnp.float32) * slope).astype(jnp.bfloat16)
        gblocks = grads.reshape(NBLKS, BLK, F).astype(jnp.float32)
        returned = jnp.einsum('kji,kjf->kif', loop_vals, gblocks[target_flat]).astype(jnp.bfloat16)
        returned = jnp.where(live_flat[:, None, None], returned, jnp.zeros((), jnp.bfloat16)).astype(jnp.float32)
        back_far = jax.ops.segment_sum(returned, source_flat, num_segments=NBLKS).reshape(BINS, F)
        grad_z = (band_apply(grads, band_vals[cell]) + back_far).astype(jnp.bfloat16)
        grads_in.append(jnp.dot(grad_z, weight.T, preferred_element_type=jnp.float32).astype(jnp.bfloat16))
        grad_weight = grad_weight + jnp.dot(inputs[cell].T, grad_z, preferred_element_type=jnp.float32)
    return (jnp.stack(outputs), jnp.stack(grads_in), grad_weight)
```

```python
import functools
import math

import jax
import jax.numpy as jnp
from jax import lax
from jax.experimental import pallas as pl
from jax.experimental.pallas import tpu as pltpu
from jax.sharding import PartitionSpec as P

BLK = 128
BAND = 4
WIDTH = 2 * BAND + 1
SLOTS_STEP = 4
ROWS_STEP = 512
VMEM_LIMIT = 48 * 1024 * 1024

band_gain = 3.0
FACTOR = band_gain / math.sqrt(WIDTH * BLK)


def dot(a, b):
    return jnp.dot(a, b, preferred_element_type=jnp.float32)


def dot_ta(a, b):
    return lax.dot_general(a, b, (((0,), (0,)), ((), ())), preferred_element_type=jnp.float32)


def dot_tb(a, b):
    return lax.dot_general(a, b, (((1,), (1,)), ((), ())), preferred_element_type=jnp.float32)


def params():
    return pltpu.CompilerParams(
        dimension_semantics=("arbitrary",), vmem_limit_bytes=VMEM_LIMIT
    )


def block_rows(index):
    return pl.ds(pl.multiple_of(index * BLK, BLK), BLK)


def gather_kernel(cap, index_ref, count_ref, x_ref, out_ref):
    step = pl.program_id(0)
    for j in range(SLOTS_STEP):
        slot = step * SLOTS_STEP + j
        live = lax.rem(slot, cap) < count_ref[slot // cap]

        @pl.when(live)
        def _():
            out_ref[pl.ds(j * BLK, BLK), :] = x_ref[block_rows(index_ref[slot]), :]

        @pl.when(jnp.logical_not(live))
        def _():
            out_ref[pl.ds(j * BLK, BLK), :] = jnp.zeros((BLK, out_ref.shape[1]), out_ref.dtype)


def gather_blocks(x, index, count, cap):
    slots = index.shape[0]
    features = x.shape[1]
    return pl.pallas_call(
        functools.partial(gather_kernel, cap),
        grid_spec=pltpu.PrefetchScalarGridSpec(
            num_scalar_prefetch=2,
            grid=(slots // SLOTS_STEP,),
            in_specs=[pl.BlockSpec(x.shape, lambda i, *_: (0, 0))],
            out_specs=pl.BlockSpec((SLOTS_STEP * BLK, features), lambda i, *_: (i, 0)),
        ),
        out_shape=jax.ShapeDtypeStruct((slots * BLK, features), x.dtype),
        compiler_params=params(),
        cost_estimate=pl.CostEstimate(
            flops=0, bytes_accessed=2 * (x.size + slots * BLK * features), transcendentals=0
        ),
        name="gather_blocks",
    )(index, count, x)


def band_kernel(low_ref, v_ref, high_ref, band_ref, out_ref, padded):
    step = pl.program_id(0)
    rim = low_ref.shape[0]
    rows = v_ref.shape[0]

    @pl.when(step == 0)
    def _():
        padded[pl.ds(0, rim), :] = low_ref[...]
        padded[pl.ds(rim, rows), :] = v_ref[...]
        padded[pl.ds(rim + rows, rim), :] = high_ref[...]

    left = jnp.concatenate([band_ref[0, d] for d in range(WIDTH)], axis=1)
    window = padded[pl.ds(pl.multiple_of(step * BLK, BLK), WIDTH * BLK), :]
    out_ref[...] = FACTOR * dot(left, window)


def band_sum(low, v, high, band):
    rows, features = v.shape
    blocks = band.shape[0]
    whole = lambda a: pl.BlockSpec(a.shape, lambda i: (0, 0))
    return pl.pallas_call(
        band_kernel,
        grid=(blocks,),
        in_specs=[
            whole(low),
            whole(v),
            whole(high),
            pl.BlockSpec((1, WIDTH, BLK, BLK), lambda i: (i, 0, 0, 0)),
        ],
        out_specs=pl.BlockSpec((BLK, features), lambda i: (i, 0)),
        out_shape=jax.ShapeDtypeStruct((rows, features), jnp.float32),
        scratch_shapes=[pltpu.VMEM((rows + 2 * low.shape[0], features), v.dtype)],
        compiler_params=params(),
        cost_estimate=pl.CostEstimate(
            flops=2 * band.size * features,
            bytes_accessed=2 * band.size + 6 * v.size,
            transcendentals=0,
        ),
        name="band_sum",
    )(low, v, high, band)


def middle_kernel(
    loop_steps,
    target_ref,
    arrived_ref,
    vals_ref,
    band_ref,
    weight_ref,
    grad_ref,
    output_ref,
    grads_ref,
    y_ref,
    total,
):
    step = pl.program_id(0)

    @pl.when(step == 0)
    def _():
        total[...] = jnp.zeros_like(total)

    @pl.when(step < loop_steps)
    def _():
        for j in range(SLOTS_STEP):
            rows = block_rows(target_ref[step * SLOTS_STEP + j])
            total[rows, :] += dot(vals_ref[j], arrived_ref[pl.ds(j * BLK, BLK), :])

    @pl.when(step >= loop_steps)
    def _():
        rows = pl.ds(pl.multiple_of((step - loop_steps) * ROWS_STEP, ROWS_STEP), ROWS_STEP)
        y = (total[rows, :] + band_ref[...]).astype(jnp.bfloat16)
        y_ref[...] = y
        preact = dot(y, weight_ref[...])
        sigma = jax.nn.sigmoid(preact)
        output_ref[...] = (preact * sigma).astype(jnp.bfloat16)
        slope = sigma * (1.0 + preact * (1.0 - sigma))
        grads_ref[...] = (grad_ref[...].astype(jnp.float32) * slope).astype(jnp.bfloat16)


def middle(target, arrived, vals, band, weight, grad_out):
    rows, features = grad_out.shape
    slots = target.shape[0]
    loop_steps = slots // SLOTS_STEP
    row_steps = rows // ROWS_STEP
    by_loop = lambda i, *_: (jnp.minimum(i, loop_steps - 1), 0)
    by_row = lambda i, *_: (jnp.maximum(i - loop_steps, 0), 0)
    row_spec = pl.BlockSpec((ROWS_STEP, features), by_row)
    out = jax.ShapeDtypeStruct((rows, features), jnp.bfloat16)
    return pl.pallas_call(
        functools.partial(middle_kernel, loop_steps),
        grid_spec=pltpu.PrefetchScalarGridSpec(
            num_scalar_prefetch=1,
            grid=(loop_steps + row_steps,),
            in_specs=[
                pl.BlockSpec((SLOTS_STEP * BLK, features), by_loop),
                pl.BlockSpec(
                    (SLOTS_STEP, BLK, BLK), lambda i, *_: (jnp.minimum(i, loop_steps - 1), 0, 0)
                ),
                row_spec,
                pl.BlockSpec(weight.shape, lambda i, *_: (0, 0)),
                row_spec,
            ],
            out_specs=[row_spec] * 3,
            scratch_shapes=[pltpu.VMEM((rows, features), jnp.float32)],
        ),
        out_shape=[out] * 3,
        compiler_params=params(),
        cost_estimate=pl.CostEstimate(
            flops=2 * (vals.size + rows * features) * features,
            bytes_accessed=2 * (arrived.size + vals.size + 6 * rows * features),
            transcendentals=rows * features,
        ),
        name="middle",
    )(target, arrived, vals, band, weight, grad_out)


def back_kernel(target_ref, grads_ref, vals_ref, out_ref):
    step = pl.program_id(0)
    for j in range(SLOTS_STEP):
        rows = block_rows(target_ref[step * SLOTS_STEP + j])
        term = dot_ta(vals_ref[j], grads_ref[rows, :])
        out_ref[pl.ds(j * BLK, BLK), :] = term.astype(jnp.bfloat16)


def back_terms(target, grads, vals):
    slots = target.shape[0]
    features = grads.shape[1]
    return pl.pallas_call(
        back_kernel,
        grid_spec=pltpu.PrefetchScalarGridSpec(
            num_scalar_prefetch=1,
            grid=(slots // SLOTS_STEP,),
            in_specs=[
                pl.BlockSpec(grads.shape, lambda i, *_: (0, 0)),
                pl.BlockSpec((SLOTS_STEP, BLK, BLK), lambda i, *_: (i, 0, 0)),
            ],
            out_specs=pl.BlockSpec((SLOTS_STEP * BLK, features), lambda i, *_: (i, 0)),
        ),
        out_shape=jax.ShapeDtypeStruct((slots * BLK, features), jnp.bfloat16),
        compiler_params=params(),
        cost_estimate=pl.CostEstimate(
            flops=2 * vals.size * features,
            bytes_accessed=2 * (slots * BLK * features + vals.size + grads.size),
            transcendentals=0,
        ),
        name="back_terms",
    )(target, grads, vals)


def tail_kernel(
    cap, loop_steps, index_ref, count_ref, back_ref, band_ref, weight_ref, out_ref, total
):
    step = pl.program_id(0)

    @pl.when(step == 0)
    def _():
        total[...] = jnp.zeros_like(total)

    @pl.when(step < loop_steps)
    def _():
        for j in range(SLOTS_STEP):
            slot = step * SLOTS_STEP + j

            @pl.when(lax.rem(slot, cap) < count_ref[slot // cap])
            def _():
                rows = block_rows(index_ref[slot])
                total[rows, :] += back_ref[pl.ds(j * BLK, BLK), :].astype(jnp.float32)

    @pl.when(step >= loop_steps)
    def _():
        rows = pl.ds(pl.multiple_of((step - loop_steps) * ROWS_STEP, ROWS_STEP), ROWS_STEP)
        grad_z = (total[rows, :] + band_ref[...]).astype(jnp.bfloat16)
        out_ref[...] = dot_tb(grad_z, weight_ref[...]).astype(jnp.bfloat16)


def tail(index, count, cap, back, band, weight):
    rows, features = band.shape
    slots = index.shape[0]
    loop_steps = slots // SLOTS_STEP
    row_steps = rows // ROWS_STEP
    row_spec = pl.BlockSpec(
        (ROWS_STEP, features), lambda i, *_: (jnp.maximum(i - loop_steps, 0), 0)
    )
    return pl.pallas_call(
        functools.partial(tail_kernel, cap, loop_steps),
        grid_spec=pltpu.PrefetchScalarGridSpec(
            num_scalar_prefetch=2,
            grid=(loop_steps + row_steps,),
            in_specs=[
                pl.BlockSpec(
                    (SLOTS_STEP * BLK, features),
                    lambda i, *_: (jnp.minimum(i, loop_steps - 1), 0),
                ),
                row_spec,
                pl.BlockSpec(weight.shape, lambda i, *_: (0, 0)),
            ],
            out_specs=row_spec,
            scratch_shapes=[pltpu.VMEM((rows, features), jnp.float32)],
        ),
        out_shape=jax.ShapeDtypeStruct((rows, features), jnp.bfloat16),
        compiler_params=params(),
        cost_estimate=pl.CostEstimate(
            flops=2 * band.size * features,
            bytes_accessed=2 * back.size + 6 * band.size,
            transcendentals=0,
        ),
        name="tail",
    )(index, count, back, band, weight)


def rims(v):
    count = lax.axis_size("genome")
    width = BAND * BLK
    forward = [(i, i + 1) for i in range(count - 1)]
    backward = [(target, source) for source, target in forward]
    low = lax.ppermute(v[v.shape[0] - width :], "genome", forward)
    high = lax.ppermute(v[:width], "genome", backward)
    return low, high


def exchange(blocks):
    peers = lax.axis_size("genome")
    cut = blocks.reshape(peers, -1, blocks.shape[-1])
    return lax.all_to_all(cut, "genome", 0, 0, tiled=True).reshape(blocks.shape)


def moved(index, kind, s):
    core, x, y = index & 1, (index >> 1) & 3, index >> 3
    if kind == "core":
        core = core ^ 1
    elif kind == "x":
        x = (x + s) & 3
    else:
        y = (y + s) & 3
    return y * 8 + x * 2 + core


def shift(v, kind, s):
    if kind == "cell":
        return lax.ppermute(v, "cell", [(i, (i + s) & 3) for i in range(4)])
    return lax.ppermute(v, "genome", [(i, moved(i, kind, s)) for i in range(32)])


def sum_everywhere(v):
    rows, columns = v.shape
    core = lax.axis_index("genome") & 1
    cell = lax.axis_index("cell")
    halves = v.reshape(2, rows // 2, columns)
    mine = lax.dynamic_index_in_dim(halves, core, 0, keepdims=False)
    other = lax.dynamic_index_in_dim(halves, 1 - core, 0, keepdims=False)
    mine = mine + shift(other, "core", 1)
    parts = mine.reshape(4, rows // 8, columns)
    total = lax.dynamic_index_in_dim(parts, cell, 0, keepdims=False)
    for s in (1, 2, 3):
        part = lax.dynamic_index_in_dim(parts, (cell + s) & 3, 0, keepdims=False)
        total = total + shift(part, "cell", s)
    for kind in ("y", "x"):
        total = total + sum(shift(total, kind, s) for s in (1, 2, 3))
    around = jnp.stack([total] + [shift(total, "cell", s) for s in (1, 2, 3)])
    full = jnp.take(around, (cell - jnp.arange(4)) & 3, axis=0).reshape(rows // 2, columns)
    other = shift(full, "core", 1)
    first = jnp.where(core == 0, full, other)
    second = jnp.where(core == 0, other, full)
    return jnp.concatenate([first, second])


def on_device(inputs, weight, band_vals, far_rows, far_send, far_count, far_vals, grad_out):
    x = inputs[0]
    band = band_vals[0]
    cap = far_send.shape[-1]
    send_index = far_send.reshape(-1)
    target_index = far_rows.reshape(-1)
    count = far_count.reshape(-1)
    vals = far_vals.reshape(-1, BLK, BLK)

    low, high = rims(x)
    arrived = exchange(gather_blocks(x, send_index, count, cap))
    band_part = band_sum(low, x, high, band)
    output, grads, y = middle(target_index, arrived, vals, band_part, weight, grad_out[0])
    low, high = rims(grads)
    came_back = exchange(back_terms(target_index, grads, vals))
    back_band = band_sum(low, grads, high, band)
    grad_weight = sum_everywhere(dot_ta(y, grads))
    grad_in = tail(send_index, count, cap, came_back, back_band, weight)
    return (output[None], grad_in[None], grad_weight)


def solution(mesh):
    return jax.shard_map(
        on_device,
        mesh=mesh,
        in_specs=(
            P("cell", "genome", None),
            P(),
            P("cell", "genome", None, None, None),
            P("cell", "genome", None, None),
            P("cell", "genome", None, None),
            P("cell", "genome", None),
            P("cell", "genome", None, None, None, None),
            P("cell", "genome", None),
        ),
        out_specs=(P("cell", "genome", None), P("cell", "genome", None), P()),
        check_vma=False,
    )
```

```python
import functools
import math

import jax
import jax.numpy as jnp
from jax import lax
from jax.experimental import pallas as pl
from jax.experimental.pallas import tpu as pltpu
from jax.sharding import PartitionSpec as P

BLK = 128
BAND = 4
WIDTH = 2 * BAND + 1
CHUNK = 16 * BLK
ROWS_STEP = 256
VMEM_LIMIT = 48 * 1024 * 1024

SMEM = pl.BlockSpec(memory_space=pltpu.SMEM)
VMEM = pl.BlockSpec(memory_space=pltpu.VMEM)
HBM = pl.BlockSpec(memory_space=pl.ANY)

band_gain = 3.0
FACTOR = band_gain / math.sqrt(WIDTH * BLK)


def dot(a, b):
    return jnp.dot(a, b, preferred_element_type=jnp.float32)


def dot_ta(a, b):
    return lax.dot_general(a, b, (((0,), (0,)), ((), ())), preferred_element_type=jnp.float32)


def dot_tb(a, b):
    return lax.dot_general(a, b, (((1,), (1,)), ((), ())), preferred_element_type=jnp.float32)


def params():
    return pltpu.CompilerParams(vmem_limit_bytes=VMEM_LIMIT)


def block_rows(index):
    return pl.ds(pl.multiple_of(index * BLK, BLK), BLK)


def gather_kernel(
    index_ref, count_ref, x_ref, out_ref, index, count, x, zeros, small_sems, in_sem, sem
):
    cap, peers = index_ref.shape
    copies = [
        pltpu.make_async_copy(index_ref, index, small_sems.at[0]),
        pltpu.make_async_copy(count_ref, count, small_sems.at[1]),
    ]
    for copy in copies:
        copy.start()
    for i in range(x.shape[0] // ROWS_STEP):
        rows = pl.ds(i * ROWS_STEP, ROWS_STEP)
        pltpu.make_async_copy(x_ref.at[rows], x.at[rows], in_sem).start()
    zeros[...] = jnp.zeros_like(zeros)
    for copy in copies:
        copy.wait()
    pltpu.make_async_copy(x_ref, x, in_sem).wait()

    def send(peer, carry):
        for s in range(cap):
            target = out_ref.at[block_rows(peer * cap + s)]
            live = s < count[0, peer]

            @pl.when(live)
            def _():
                pltpu.make_async_copy(x.at[block_rows(index[s, peer])], target, sem).start()

            @pl.when(jnp.logical_not(live))
            def _():
                pltpu.make_async_copy(zeros, target, sem).start()

        return carry

    lax.fori_loop(0, peers, send, 0)
    pltpu.make_async_copy(out_ref, out_ref, sem).wait()


def gather_blocks(x, index, count):
    cap, peers = index.shape
    features = x.shape[1]
    return pl.pallas_call(
        gather_kernel,
        in_specs=[HBM] * 3,
        out_specs=HBM,
        out_shape=jax.ShapeDtypeStruct((peers * cap * BLK, features), x.dtype),
        scratch_shapes=[
            pltpu.SMEM(index.shape, index.dtype),
            pltpu.SMEM(count.shape, count.dtype),
            pltpu.VMEM(x.shape, x.dtype),
            pltpu.VMEM((BLK, features), x.dtype),
            pltpu.SemaphoreType.DMA((2,)),
            pltpu.SemaphoreType.DMA,
            pltpu.SemaphoreType.DMA,
        ],
        compiler_params=params(),
        cost_estimate=pl.CostEstimate(
            flops=0,
            bytes_accessed=2 * (x.size + peers * cap * BLK * features),
            transcendentals=0,
        ),
        name="gather_blocks",
    )(index, count, x)


def band_kernel(v_ref, band_ref, out_ref, padded, kept, sem):
    step = pl.program_id(0)
    rim = BAND * BLK
    rows, features = v_ref.shape

    @pl.when(step == 0)
    def _():
        padded[pl.ds(0, rim), :] = jnp.zeros((rim, features), padded.dtype)
        padded[pl.ds(rim, rows), :] = v_ref[...]
        padded[pl.ds(rim + rows, rim), :] = jnp.zeros((rim, features), padded.dtype)

    left = jnp.concatenate([band_ref[0, d] for d in range(WIDTH)], axis=1)
    window = padded[pl.ds(pl.multiple_of(step * BLK, BLK), WIDTH * BLK), :]
    rows = block_rows(step)
    kept[rows, :] = FACTOR * dot(left, window)
    pltpu.make_async_copy(kept.at[rows], out_ref.at[rows], sem).start()

    @pl.when(step == pl.num_programs(0) - 1)
    def _():
        pltpu.make_async_copy(kept, out_ref, sem).wait()


def band_sum(v, band):
    rows, features = v.shape
    return pl.pallas_call(
        band_kernel,
        grid=(band.shape[0],),
        in_specs=[
            pl.BlockSpec(v.shape, lambda i: (0, 0)),
            pl.BlockSpec((1, WIDTH, BLK, BLK), lambda i: (i, 0, 0, 0)),
        ],
        out_specs=HBM,
        out_shape=jax.ShapeDtypeStruct((rows, features), jnp.float32),
        scratch_shapes=[
            pltpu.VMEM((rows + 2 * BAND * BLK, features), v.dtype),
            pltpu.VMEM((rows, features), jnp.float32),
            pltpu.SemaphoreType.DMA,
        ],
        compiler_params=params(),
        cost_estimate=pl.CostEstimate(
            flops=2 * band.size * features,
            bytes_accessed=2 * band.size + 6 * v.size,
            transcendentals=0,
        ),
        name="band_sum",
    )(v, band)


def rim_kernel(v_ref, first_ref, last_ref, low_ref, high_ref):
    start = v_ref.shape[0] - BAND * BLK
    for m in range(BAND):
        rows = pl.ds(m * BLK, BLK)
        left = jnp.concatenate([first_ref[j, m - j] for j in range(m + 1)], axis=0)
        term = dot_ta(left, v_ref[pl.ds(0, (m + 1) * BLK), :])
        low_ref[rows, :] = (FACTOR * term).astype(low_ref.dtype)
        left = jnp.concatenate([last_ref[j, 2 * BAND + m - j] for j in range(m, BAND)], axis=0)
        term = dot_ta(left, v_ref[pl.ds(start + m * BLK, (BAND - m) * BLK), :])
        high_ref[rows, :] = (FACTOR * term).astype(high_ref.dtype)


def rim_terms(v, band):
    blocks = band.shape[0]
    features = v.shape[1]
    part = (BAND,) + band.shape[1:]
    out = jax.ShapeDtypeStruct((BAND * BLK, features), v.dtype)
    return pl.pallas_call(
        rim_kernel,
        grid=(1,),
        in_specs=[
            pl.BlockSpec(v.shape, lambda i: (0, 0)),
            pl.BlockSpec(part, lambda i: (0, 0, 0, 0)),
            pl.BlockSpec(part, lambda i: (blocks // BAND - 1, 0, 0, 0)),
        ],
        out_specs=[pl.BlockSpec(out.shape, lambda i: (0, 0))] * 2,
        out_shape=[out] * 2,
        compiler_params=params(),
        cost_estimate=pl.CostEstimate(
            flops=2 * 20 * BLK * BLK * features, bytes_accessed=6 << 20, transcendentals=0
        ),
        name="rim_terms",
    )(v, band, band)


def neighbour_terms(v, band):
    count = lax.axis_size("genome")
    forward = [(i, i + 1) for i in range(count - 1)]
    backward = [(target, source) for source, target in forward]
    low, high = rim_terms(v, band)
    return lax.ppermute(high, "genome", forward), lax.ppermute(low, "genome", backward)


def start_total(total, band_ref, low_ref, high_ref):
    rows = total.shape[0]
    rim = low_ref.shape[0]
    total[pl.ds(0, rim), :] = band_ref[pl.ds(0, rim), :] + low_ref[...].astype(jnp.float32)
    total[pl.ds(rim, rows - 2 * rim), :] = band_ref[pl.ds(rim, rows - 2 * rim), :]
    total[pl.ds(rows - rim, rim), :] = band_ref[pl.ds(rows - rim, rim), :] + high_ref[
        ...
    ].astype(jnp.float32)


def middle_kernel(
    target_ref,
    arrived_ref,
    vals_ref,
    band_ref,
    low_ref,
    high_ref,
    weight_ref,
    grad_ref,
    output_ref,
    grads_ref,
    y_ref,
    terms_ref,
    blocks,
    total,
    kept,
    in_sems,
    out_sems,
):
    chunks = blocks.shape[0] // CHUNK
    slots = CHUNK // BLK
    steps = total.shape[0] // ROWS_STEP
    for i in range(chunks):
        rows = pl.ds(i * CHUNK, CHUNK)
        pltpu.make_async_copy(arrived_ref.at[rows], blocks.at[rows], in_sems.at[i]).start()
    start_total(total, band_ref, low_ref, high_ref)

    def add_chunk(i, carry):
        rows = pl.ds(pl.multiple_of(i * CHUNK, CHUNK), CHUNK)
        pltpu.make_async_copy(arrived_ref.at[rows], blocks.at[rows], in_sems.at[i]).wait()
        for j in range(slots):
            slot = i * slots + j
            rows = block_rows(target_ref[slot])
            total[rows, :] += dot(vals_ref[slot], blocks[block_rows(slot), :])
        return carry

    lax.fori_loop(0, chunks, add_chunk, 0)

    outs = (output_ref, grads_ref, y_ref)
    for i in range(steps):
        rows = pl.ds(i * ROWS_STEP, ROWS_STEP)
        y = total[rows, :].astype(jnp.bfloat16)
        kept[2, rows, :] = y
        preact = dot(y, weight_ref[...])
        sigma = jax.nn.sigmoid(preact)
        kept[0, rows, :] = (preact * sigma).astype(jnp.bfloat16)
        slope = sigma * (1.0 + preact * (1.0 - sigma))
        kept[1, rows, :] = (grad_ref[rows, :].astype(jnp.float32) * slope).astype(jnp.bfloat16)
        for k in range(3):
            pltpu.make_async_copy(kept.at[k, rows], outs[k].at[rows], out_sems.at[k]).start()

    def back_chunk(i, carry):
        for j in range(slots):
            slot = i * slots + j
            rows = block_rows(target_ref[slot])
            term = dot_ta(vals_ref[slot], kept[1, rows, :])
            blocks[block_rows(slot), :] = term.astype(jnp.bfloat16)
        rows = pl.ds(pl.multiple_of(i * CHUNK, CHUNK), CHUNK)
        pltpu.make_async_copy(blocks.at[rows], terms_ref.at[rows], out_sems.at[3]).start()
        return carry

    lax.fori_loop(0, chunks, back_chunk, 0)
    for k in range(3):
        pltpu.make_async_copy(kept.at[k], outs[k], out_sems.at[k]).wait()
    pltpu.make_async_copy(blocks, terms_ref, out_sems.at[3]).wait()


def middle(target, arrived, vals, band, low, high, weight, grad_out):
    rows, features = grad_out.shape
    out = jax.ShapeDtypeStruct((rows, features), jnp.bfloat16)
    return pl.pallas_call(
        middle_kernel,
        in_specs=[SMEM, HBM] + [VMEM] * 6,
        out_specs=[HBM] * 4,
        out_shape=[out] * 3 + [jax.ShapeDtypeStruct(arrived.shape, jnp.bfloat16)],
        scratch_shapes=[
            pltpu.VMEM(arrived.shape, jnp.bfloat16),
            pltpu.VMEM((rows, features), jnp.float32),
            pltpu.VMEM((3, rows, features), jnp.bfloat16),
            pltpu.SemaphoreType.DMA((arrived.shape[0] // CHUNK,)),
            pltpu.SemaphoreType.DMA((4,)),
        ],
        compiler_params=params(),
        cost_estimate=pl.CostEstimate(
            flops=2 * (2 * vals.size + rows * features) * features,
            bytes_accessed=2 * (2 * arrived.size + vals.size + 6 * rows * features),
            transcendentals=rows * features,
        ),
        name="middle",
    )(target, arrived, vals, band, low, high, weight, grad_out)


def tail_kernel(
    cap,
    index_ref,
    count_ref,
    back_ref,
    band_ref,
    low_ref,
    high_ref,
    weight_ref,
    out_ref,
    back,
    total,
    kept,
    in_sems,
    sem,
):
    chunks = back_ref.shape[0] // CHUNK
    steps = total.shape[0] // ROWS_STEP
    for i in range(chunks):
        rows = pl.ds(i * CHUNK, CHUNK)
        pltpu.make_async_copy(back_ref.at[rows], back.at[rows], in_sems.at[i]).start()
    start_total(total, band_ref, low_ref, high_ref)

    def add_chunk(i, carry):
        rows = pl.ds(pl.multiple_of(i * CHUNK, CHUNK), CHUNK)
        pltpu.make_async_copy(back_ref.at[rows], back.at[rows], in_sems.at[i]).wait()
        for j in range(CHUNK // BLK):
            slot = i * (CHUNK // BLK) + j

            @pl.when(lax.rem(slot, cap) < count_ref[slot // cap])
            def _():
                rows = block_rows(index_ref[slot])
                total[rows, :] += back[block_rows(slot), :].astype(jnp.float32)

        return carry

    lax.fori_loop(0, chunks, add_chunk, 0)
    for i in range(steps):
        rows = pl.ds(i * ROWS_STEP, ROWS_STEP)
        grad_z = total[rows, :].astype(jnp.bfloat16)
        kept[rows, :] = dot(grad_z, weight_ref[...]).astype(jnp.bfloat16)
        pltpu.make_async_copy(kept.at[rows], out_ref.at[rows], sem).start()
    pltpu.make_async_copy(kept, out_ref, sem).wait()


def tail(index, count, cap, back, band, low, high, weight_t):
    rows, features = band.shape
    return pl.pallas_call(
        functools.partial(tail_kernel, cap),
        in_specs=[SMEM, SMEM, HBM] + [VMEM] * 4,
        out_specs=HBM,
        out_shape=jax.ShapeDtypeStruct((rows, features), jnp.bfloat16),
        scratch_shapes=[
            pltpu.VMEM(back.shape, jnp.bfloat16),
            pltpu.VMEM((rows, features), jnp.float32),
            pltpu.VMEM((rows, features), jnp.bfloat16),
            pltpu.SemaphoreType.DMA((back.shape[0] // CHUNK,)),
            pltpu.SemaphoreType.DMA,
        ],
        compiler_params=params(),
        cost_estimate=pl.CostEstimate(
            flops=2 * band.size * features,
            bytes_accessed=2 * back.size + 6 * band.size,
            transcendentals=0,
        ),
        name="tail",
    )(index, count, back, band, low, high, weight_t)


def exchange(blocks):
    peers = lax.axis_size("genome")
    cut = blocks.reshape(peers, -1, blocks.shape[-1])
    return lax.all_to_all(cut, "genome", 0, 0, tiled=True).reshape(blocks.shape)


def moved(index, kind, s):
    core, x, y = index & 1, (index >> 1) & 3, index >> 3
    if kind == "x":
        x = (x + s) & 3
    else:
        y = (y + s) & 3
    return y * 8 + x * 2 + core


def shift(v, kind, s):
    return lax.ppermute(v, "genome", [(i, moved(i, kind, s)) for i in range(32)])


def within(v, flip, s):
    pairs = [
        (g * 4 + c, (g ^ flip) * 4 + ((c + s) & 3)) for g in range(32) for c in range(4)
    ]
    return lax.ppermute(v, ("genome", "cell"), pairs)


def scatter_sum(v, core, cell):
    rows = v.shape[0] // 8
    total = None
    for flip in (0, 1):
        for s in range(4):
            owner = (core ^ flip) * 4 + ((cell + s) & 3)
            part = lax.dynamic_slice_in_dim(v, owner * rows, rows, axis=0)
            part = part if (flip, s) == (0, 0) else within(part, flip, s)
            total = part if total is None else total + part
    return total


def put_kernel(cell_ref, *refs):
    out_ref = refs[-1]
    rows = refs[0].shape[0]
    for s, ref in enumerate(refs[:-1]):
        place = ((cell_ref[0] - s) & 3) * rows
        out_ref[pl.ds(pl.multiple_of(place, rows), rows), :] = ref[...]


def join_kernel(core_ref, mine_ref, other_ref, out_ref):
    rows = mine_ref.shape[0]
    for ref, core in ((mine_ref, core_ref[0]), (other_ref, 1 - core_ref[0])):
        out_ref[pl.ds(pl.multiple_of(core * rows, rows), rows), :] = ref[...].astype(
            jnp.float32
        )


def gather_sum(v, core, cell):
    rows, features = v.shape
    parts = [v] + [within(v, 0, s) for s in (1, 2, 3)]
    mine = pl.pallas_call(
        put_kernel,
        in_specs=[SMEM] + [VMEM] * 4,
        out_specs=VMEM,
        out_shape=jax.ShapeDtypeStruct((4 * rows, features), v.dtype),
        compiler_params=params(),
        name="put_parts",
    )(cell[None], *parts)
    return pl.pallas_call(
        join_kernel,
        in_specs=[SMEM] + [VMEM] * 2,
        out_specs=VMEM,
        out_shape=jax.ShapeDtypeStruct((8 * rows, features), jnp.float32),
        compiler_params=params(),
        name="join_halves",
    )(core[None], mine, within(mine, 1, 0))


def on_device(inputs, weight, band_vals, far_rows, far_send, far_count, far_vals, grad_out):
    x = inputs[0]
    band = band_vals[0]
    cap = far_send.shape[-1]
    send_index = far_send.reshape(-1)
    target_index = far_rows.reshape(-1)
    count = far_count.reshape(-1)
    vals = far_vals.reshape(-1, BLK, BLK)
    core = lax.axis_index("genome") & 1
    cell = lax.axis_index("cell")

    arrived = exchange(gather_blocks(x, far_send[0, 0].T, far_count[0]))
    low, high = neighbour_terms(x, band)
    band_part = band_sum(x, band)
    output, grads, y, terms = middle(
        target_index, arrived, vals, band_part, low, high, weight, grad_out[0]
    )
    came_back = exchange(terms)
    low, high = neighbour_terms(grads, band)
    part = scatter_sum(dot_ta(y, grads), core, cell)
    back_band = band_sum(grads, band)
    part, back_band = lax.optimization_barrier((part, back_band))
    sent = part.astype(jnp.bfloat16)
    part = part + sum(shift(sent, "y", s).astype(jnp.float32) for s in (1, 2, 3))
    sent = part.astype(jnp.bfloat16)
    moved_on = [shift(sent, "x", s) for s in (1, 2, 3)]
    grad_in = tail(send_index, count, cap, came_back, back_band, low, high, weight.T)
    moved_on, grad_in = lax.optimization_barrier((moved_on, grad_in))
    part = part + sum(v.astype(jnp.float32) for v in moved_on)
    grad_weight = gather_sum(part.astype(jnp.bfloat16), core, cell)
    return (output[None], grad_in[None], grad_weight)


def solution(mesh):
    return jax.shard_map(
        on_device,
        mesh=mesh,
        in_specs=(
            P("cell", "genome", None),
            P(),
            P("cell", "genome", None, None, None),
            P("cell", "genome", None, None),
            P("cell", "genome", None, None),
            P("cell", "genome", None),
            P("cell", "genome", None, None, None, None),
            P("cell", "genome", None),
        ),
        out_specs=(P("cell", "genome", None), P("cell", "genome", None), P()),
        check_vma=False,
    )
```

```python
import functools
import math

import jax
import jax.numpy as jnp
from jax import lax
from jax.experimental import pallas as pl
from jax.experimental.pallas import tpu as pltpu
from jax.sharding import PartitionSpec as P

BLK = 128
BAND = 4
WIDTH = 2 * BAND + 1
CHUNK = 16 * BLK
ROWS_STEP = 256
VMEM_LIMIT = 65_400_000

SMEM = pl.BlockSpec(memory_space=pltpu.SMEM)
VMEM = pl.BlockSpec(memory_space=pltpu.VMEM)
HBM = pl.BlockSpec(memory_space=pltpu.HBM)
ANY = pl.BlockSpec(memory_space=pl.ANY)

band_gain = 3.0
FACTOR = band_gain / math.sqrt(WIDTH * BLK)


def dot(a, b):
    return jnp.dot(a, b, preferred_element_type=jnp.float32)


def dot_ta(a, b):
    return lax.dot_general(a, b, (((0,), (0,)), ((), ())), preferred_element_type=jnp.float32)


def dot_tb(a, b):
    return lax.dot_general(a, b, (((1,), (1,)), ((), ())), preferred_element_type=jnp.float32)


def params():
    return pltpu.CompilerParams(vmem_limit_bytes=VMEM_LIMIT)


def block_rows(index):
    return pl.ds(pl.multiple_of(index * BLK, BLK), BLK)


def gather_kernel(
    index_ref, count_ref, x_ref, out_ref, index, count, x, zeros, small_sems, in_sem, sem
):
    cap, peers = index_ref.shape
    copies = [
        pltpu.make_async_copy(index_ref, index, small_sems.at[0]),
        pltpu.make_async_copy(count_ref, count, small_sems.at[1]),
    ]
    for copy in copies:
        copy.start()
    for i in range(x.shape[0] // ROWS_STEP):
        rows = pl.ds(i * ROWS_STEP, ROWS_STEP)
        pltpu.make_async_copy(x_ref.at[rows], x.at[rows], in_sem).start()
    zeros[...] = jnp.zeros_like(zeros)
    for copy in copies:
        copy.wait()
    pltpu.make_async_copy(x_ref, x, in_sem).wait()

    def send(peer, carry):
        for s in range(cap):
            target = out_ref.at[block_rows(peer * cap + s)]
            live = s < count[0, peer]

            @pl.when(live)
            def _():
                pltpu.make_async_copy(x.at[block_rows(index[s, peer])], target, sem).start()

            @pl.when(jnp.logical_not(live))
            def _():
                pltpu.make_async_copy(zeros, target, sem).start()

        return carry

    lax.fori_loop(0, peers, send, 0)
    pltpu.make_async_copy(out_ref, out_ref, sem).wait()


def gather_blocks(x, index, count):
    cap, peers = index.shape
    features = x.shape[1]
    return pl.pallas_call(
        gather_kernel,
        in_specs=[HBM] * 3,
        out_specs=HBM,
        out_shape=jax.ShapeDtypeStruct((peers * cap * BLK, features), x.dtype),
        scratch_shapes=[
            pltpu.SMEM(index.shape, index.dtype),
            pltpu.SMEM(count.shape, count.dtype),
            pltpu.VMEM(x.shape, x.dtype),
            pltpu.VMEM((BLK, features), x.dtype),
            pltpu.SemaphoreType.DMA((2,)),
            pltpu.SemaphoreType.DMA,
            pltpu.SemaphoreType.DMA,
        ],
        compiler_params=params(),
        cost_estimate=pl.CostEstimate(
            flops=0,
            bytes_accessed=2 * (x.size + peers * cap * BLK * features),
            transcendentals=0,
        ),
        name="gather_blocks",
    )(index, count, x)


def band_kernel(v_ref, band_ref, out_ref, padded, kept, sem):
    step = pl.program_id(0)
    rim = BAND * BLK
    rows, features = v_ref.shape

    @pl.when(step == 0)
    def _():
        padded[pl.ds(0, rim), :] = jnp.zeros((rim, features), padded.dtype)
        padded[pl.ds(rim, rows), :] = v_ref[...]
        padded[pl.ds(rim + rows, rim), :] = jnp.zeros((rim, features), padded.dtype)

    left = jnp.concatenate([band_ref[0, d] for d in range(WIDTH)], axis=1)
    window = padded[pl.ds(pl.multiple_of(step * BLK, BLK), WIDTH * BLK), :]
    rows = block_rows(step)
    kept[rows, :] = FACTOR * dot(left, window)
    pltpu.make_async_copy(kept.at[rows], out_ref.at[rows], sem).start()

    @pl.when(step == pl.num_programs(0) - 1)
    def _():
        pltpu.make_async_copy(kept, out_ref, sem).wait()


def band_sum(v, band):
    rows, features = v.shape
    return pl.pallas_call(
        band_kernel,
        grid=(band.shape[0],),
        in_specs=[
            pl.BlockSpec(v.shape, lambda i: (0, 0)),
            pl.BlockSpec((1, WIDTH, BLK, BLK), lambda i: (i, 0, 0, 0)),
        ],
        out_specs=ANY,
        out_shape=jax.ShapeDtypeStruct((rows, features), jnp.float32),
        scratch_shapes=[
            pltpu.VMEM((rows + 2 * BAND * BLK, features), v.dtype),
            pltpu.VMEM((rows, features), jnp.float32),
            pltpu.SemaphoreType.DMA,
        ],
        compiler_params=params(),
        cost_estimate=pl.CostEstimate(
            flops=2 * band.size * features,
            bytes_accessed=2 * band.size + 6 * v.size,
            transcendentals=0,
        ),
        name="band_sum",
    )(v, band)


def rim_kernel(v_ref, first_ref, last_ref, low_ref, high_ref):
    start = v_ref.shape[0] - BAND * BLK
    for m in range(BAND):
        rows = pl.ds(m * BLK, BLK)
        left = jnp.concatenate([first_ref[j, m - j] for j in range(m + 1)], axis=0)
        term = dot_ta(left, v_ref[pl.ds(0, (m + 1) * BLK), :])
        low_ref[rows, :] = (FACTOR * term).astype(low_ref.dtype)
        left = jnp.concatenate([last_ref[j, 2 * BAND + m - j] for j in range(m, BAND)], axis=0)
        term = dot_ta(left, v_ref[pl.ds(start + m * BLK, (BAND - m) * BLK), :])
        high_ref[rows, :] = (FACTOR * term).astype(high_ref.dtype)


def rim_terms(v, band):
    blocks = band.shape[0]
    features = v.shape[1]
    part = (BAND,) + band.shape[1:]
    out = jax.ShapeDtypeStruct((BAND * BLK, features), v.dtype)
    return pl.pallas_call(
        rim_kernel,
        grid=(1,),
        in_specs=[
            pl.BlockSpec(v.shape, lambda i: (0, 0)),
            pl.BlockSpec(part, lambda i: (0, 0, 0, 0)),
            pl.BlockSpec(part, lambda i: (blocks // BAND - 1, 0, 0, 0)),
        ],
        out_specs=[pl.BlockSpec(out.shape, lambda i: (0, 0))] * 2,
        out_shape=[out] * 2,
        compiler_params=params(),
        cost_estimate=pl.CostEstimate(
            flops=2 * 20 * BLK * BLK * features, bytes_accessed=6 << 20, transcendentals=0
        ),
        name="rim_terms",
    )(v, band, band)


def to_neighbours(low, high):
    count = lax.axis_size("genome")
    forward = [(i, i + 1) for i in range(count - 1)]
    backward = [(target, source) for source, target in forward]
    return lax.ppermute(high, "genome", forward), lax.ppermute(low, "genome", backward)


def fetches(sources, targets, sems):
    copies = [
        pltpu.make_async_copy(source, target, sems.at[k])
        for k, (source, target) in enumerate(zip(sources, targets))
    ]
    for copy in copies:
        copy.start()
    return copies


def chunk_copy(source, target, sems, i):
    rows = pl.ds(i * CHUNK, CHUNK)
    return pltpu.make_async_copy(source.at[rows], target.at[rows], sems.at[i])


def send_terms(s, cap, target_ref, grads, vals, blocks, terms_ref, sem):
    peers = terms_ref.shape[0] // BLK
    group = CHUNK // BLK

    def chunk(i, carry):
        for j in range(group):
            peer = i * group + j
            slot = peer * cap + s
            term = dot_ta(vals[slot], grads[block_rows(target_ref[slot]), :])
            blocks[block_rows(peer), :] = term.astype(jnp.bfloat16)
            if j % 4 == 3:
                rows = pl.ds(pl.multiple_of((peer - 3) * BLK, 4 * BLK), 4 * BLK)
                pltpu.make_async_copy(blocks.at[rows], terms_ref.at[rows], sem).start()
        return carry

    lax.fori_loop(0, peers // group, chunk, 0)


def middle_kernel(
    cap,
    target_ref,
    arrived_ref,
    vals_ref,
    band_ref,
    low_ref,
    high_ref,
    weight_ref,
    grad_ref,
    output_ref,
    grads_ref,
    y_ref,
    terms_ref,
    blocks,
    vals,
    total,
    low,
    high,
    weight,
    grad,
    kept,
    block_sems,
    sems,
    out_sems,
):
    chunks = blocks.shape[0] // CHUNK
    slots = CHUNK // BLK
    count = total.shape[0]
    steps = count // ROWS_STEP
    rim = low.shape[0]
    first = fetches((band_ref, vals_ref), (total, vals), sems)
    for i in range(chunks):
        chunk_copy(arrived_ref, blocks, block_sems, i).start()
    later = fetches(
        (low_ref, high_ref, weight_ref, grad_ref), (low, high, weight, grad), sems.at[pl.ds(2, 4)]
    )
    for copy in first:
        copy.wait()

    def add_chunk(i, carry):
        rows = pl.ds(pl.multiple_of(i * CHUNK, CHUNK), CHUNK)
        pltpu.make_async_copy(arrived_ref.at[rows], blocks.at[rows], block_sems.at[i]).wait()
        for j in range(slots):
            slot = i * slots + j
            rows = block_rows(target_ref[slot])
            total[rows, :] += dot(vals[slot], blocks[block_rows(slot), :])
        return carry

    lax.fori_loop(0, chunks, add_chunk, 0)
    for copy in later:
        copy.wait()

    outs = (output_ref, grads_ref, y_ref)
    for i in range(steps):
        start = i * ROWS_STEP
        rows = pl.ds(start, ROWS_STEP)
        summed = total[rows, :]
        if start < rim:
            summed = summed + low[rows, :].astype(jnp.float32)
        if start >= count - rim:
            edge = pl.ds(start - (count - rim), ROWS_STEP)
            summed = summed + high[edge, :].astype(jnp.float32)
        y = summed.astype(jnp.bfloat16)
        kept[2, rows, :] = y
        preact = dot(y, weight[...])
        sigma = jax.nn.sigmoid(preact)
        kept[0, rows, :] = (preact * sigma).astype(jnp.bfloat16)
        slope = sigma * (1.0 + preact * (1.0 - sigma))
        kept[1, rows, :] = (grad[rows, :].astype(jnp.float32) * slope).astype(jnp.bfloat16)
        for k in range(3):
            pltpu.make_async_copy(kept.at[k, rows], outs[k].at[rows], out_sems.at[k]).start()

    send_terms(0, cap, target_ref, kept.at[1], vals, blocks, terms_ref, out_sems.at[3])
    for k in range(3):
        pltpu.make_async_copy(kept.at[k], outs[k], out_sems.at[k]).wait()
    pltpu.make_async_copy(terms_ref, terms_ref, out_sems.at[3]).wait()


def middle(cap, target, arrived, vals, band, low, high, weight, grad_out):
    rows, features = grad_out.shape
    out = jax.ShapeDtypeStruct((rows, features), jnp.bfloat16)
    same = lambda v: pltpu.VMEM(v.shape, v.dtype)
    return pl.pallas_call(
        functools.partial(middle_kernel, cap),
        in_specs=[SMEM] + [HBM] * 3 + [ANY] * 2 + [HBM] * 2,
        out_specs=[HBM] * 4,
        out_shape=[out] * 3 + [jax.ShapeDtypeStruct((arrived.shape[0] // cap, features), jnp.bfloat16)],
        scratch_shapes=[
            *(same(v) for v in (arrived, vals, band, low, high, weight, grad_out)),
            pltpu.VMEM((3, rows, features), jnp.bfloat16),
            pltpu.SemaphoreType.DMA((arrived.shape[0] // CHUNK,)),
            pltpu.SemaphoreType.DMA((6,)),
            pltpu.SemaphoreType.DMA((4,)),
        ],
        compiler_params=params(),
        cost_estimate=pl.CostEstimate(
            flops=2 * (2 * vals.size + rows * features) * features,
            bytes_accessed=2 * (2 * arrived.size + vals.size + 6 * rows * features),
            transcendentals=rows * features,
        ),
        name="middle",
    )(target, arrived, vals, band, low, high, weight, grad_out)


def back_kernel(s, cap, target_ref, grads_ref, vals_ref, terms_ref, grads, vals, blocks, sems, sem):
    for copy in fetches((grads_ref, vals_ref), (grads, vals), sems):
        copy.wait()
    send_terms(s, cap, target_ref, grads, vals, blocks, terms_ref, sem)
    pltpu.make_async_copy(blocks, terms_ref, sem).wait()


def back_terms(s, cap, target, grads, vals):
    shape = (vals.shape[0] // cap * BLK, grads.shape[1])
    return pl.pallas_call(
        functools.partial(back_kernel, s, cap),
        in_specs=[SMEM, HBM, HBM],
        out_specs=HBM,
        out_shape=jax.ShapeDtypeStruct(shape, jnp.bfloat16),
        scratch_shapes=[
            pltpu.VMEM(grads.shape, grads.dtype),
            pltpu.VMEM(vals.shape, vals.dtype),
            pltpu.VMEM(shape, jnp.bfloat16),
            pltpu.SemaphoreType.DMA((2,)),
            pltpu.SemaphoreType.DMA,
        ],
        compiler_params=params(),
        cost_estimate=pl.CostEstimate(
            flops=2 * vals.size * shape[1] // cap, bytes_accessed=8 << 20, transcendentals=0
        ),
        name="back_terms",
    )(target, grads, vals)


def add_back(s, cap, index_ref, count_ref, back_ref, back, sems, total):
    group = CHUNK // BLK

    def chunk(i, carry):
        rows = pl.ds(pl.multiple_of(i * CHUNK, CHUNK), CHUNK)
        pltpu.make_async_copy(back_ref.at[rows], back.at[rows], sems.at[i]).wait()
        for j in range(group):
            peer = i * group + j

            @pl.when(s < count_ref[peer])
            def _():
                rows = block_rows(index_ref[peer * cap + s])
                total[rows, :] += back[block_rows(peer), :].astype(jnp.float32)

        return carry

    lax.fori_loop(0, back.shape[0] // CHUNK, chunk, 0)


def sum_kernel(
    s,
    cap,
    index_ref,
    count_ref,
    back_ref,
    band_ref,
    low_ref,
    high_ref,
    out_ref,
    back,
    total,
    low,
    high,
    sems,
    sem,
):
    rim = low.shape[0]
    first = fetches((band_ref, low_ref, high_ref), (total, low, high), sem)
    for i in range(back.shape[0] // CHUNK):
        chunk_copy(back_ref, back, sems, i).start()
    for copy in first:
        copy.wait()
    total[pl.ds(0, rim), :] += low[...].astype(jnp.float32)
    total[pl.ds(total.shape[0] - rim, rim), :] += high[...].astype(jnp.float32)
    add_back(s, cap, index_ref, count_ref, back_ref, back, sems, total)
    out = pltpu.make_async_copy(total, out_ref, sem.at[0])
    out.start()
    out.wait()


def sum_back(s, cap, index, count, back, band, low, high):
    return pl.pallas_call(
        functools.partial(sum_kernel, s, cap),
        in_specs=[SMEM] * 2 + [HBM] * 2 + [ANY] * 2,
        out_specs=HBM,
        out_shape=jax.ShapeDtypeStruct(band.shape, jnp.float32),
        scratch_shapes=[
            *(pltpu.VMEM(v.shape, v.dtype) for v in (back, band, low, high)),
            pltpu.SemaphoreType.DMA((back.shape[0] // CHUNK,)),
            pltpu.SemaphoreType.DMA((3,)),
        ],
        compiler_params=params(),
        cost_estimate=pl.CostEstimate(
            flops=band.size, bytes_accessed=12 << 20, transcendentals=0
        ),
        name="sum_back",
    )(index, count, back, band, low, high)


def tail_kernel(
    s,
    cap,
    index_ref,
    count_ref,
    back_ref,
    sum_ref,
    weight_ref,
    out_ref,
    back,
    total,
    weight,
    kept,
    back_sems,
    sems,
    sem,
):
    first = fetches((sum_ref,), (total,), sems)
    for i in range(back.shape[0] // CHUNK):
        chunk_copy(back_ref, back, back_sems, i).start()
    later = fetches((weight_ref,), (weight,), sems.at[pl.ds(1, 1)])
    for copy in first:
        copy.wait()
    add_back(s, cap, index_ref, count_ref, back_ref, back, back_sems, total)
    for copy in later:
        copy.wait()
    for i in range(total.shape[0] // ROWS_STEP):
        rows = pl.ds(i * ROWS_STEP, ROWS_STEP)
        grad_z = total[rows, :].astype(jnp.bfloat16)
        kept[rows, :] = dot(grad_z, weight[...]).astype(jnp.bfloat16)
        pltpu.make_async_copy(kept.at[rows], out_ref.at[rows], sem).start()
    pltpu.make_async_copy(kept, out_ref, sem).wait()


def tail(s, cap, index, count, back, so_far, weight_t):
    same = lambda v: pltpu.VMEM(v.shape, v.dtype)
    return pl.pallas_call(
        functools.partial(tail_kernel, s, cap),
        in_specs=[SMEM] * 2 + [HBM] * 3,
        out_specs=HBM,
        out_shape=jax.ShapeDtypeStruct(so_far.shape, jnp.bfloat16),
        scratch_shapes=[
            *(same(v) for v in (back, so_far, weight_t)),
            pltpu.VMEM(so_far.shape, jnp.bfloat16),
            pltpu.SemaphoreType.DMA((back.shape[0] // CHUNK,)),
            pltpu.SemaphoreType.DMA((2,)),
            pltpu.SemaphoreType.DMA,
        ],
        compiler_params=params(),
        cost_estimate=pl.CostEstimate(
            flops=2 * so_far.size * weight_t.shape[1],
            bytes_accessed=2 * back.size + 6 * so_far.size,
            transcendentals=0,
        ),
        name="tail",
    )(index, count, back, so_far, weight_t)


def exchange(blocks):
    peers = lax.axis_size("genome")
    cut = blocks.reshape(peers, -1, blocks.shape[-1])
    return lax.all_to_all(cut, "genome", 0, 0, tiled=True).reshape(blocks.shape)


def moved(index, kind, s):
    core, x, y = index & 1, (index >> 1) & 3, index >> 3
    if kind == "x":
        x = (x + s) & 3
    else:
        y = (y + s) & 3
    return y * 8 + x * 2 + core


def shift(v, kind, s):
    return lax.ppermute(v, "genome", [(i, moved(i, kind, s)) for i in range(32)])


def within(v, flip, s):
    pairs = [
        (g * 4 + c, (g ^ flip) * 4 + ((c + s) & 3)) for g in range(32) for c in range(4)
    ]
    return lax.ppermute(v, ("genome", "cell"), pairs)


def scatter_sum(v, core, cell):
    rows = v.shape[0] // 8
    total = None
    for flip in (0, 1):
        for s in range(4):
            owner = (core ^ flip) * 4 + ((cell + s) & 3)
            part = lax.dynamic_slice_in_dim(v, owner * rows, rows, axis=0)
            part = part if (flip, s) == (0, 0) else within(part, flip, s)
            total = part if total is None else total + part
    return total


def put_kernel(cell_ref, *refs):
    out_ref = refs[-1]
    rows = refs[0].shape[0]
    for s, ref in enumerate(refs[:-1]):
        place = ((cell_ref[0] - s) & 3) * rows
        out_ref[pl.ds(pl.multiple_of(place, rows), rows), :] = ref[...]


def join_kernel(core_ref, mine_ref, other_ref, out_ref):
    rows = mine_ref.shape[0]
    for ref, core in ((mine_ref, core_ref[0]), (other_ref, 1 - core_ref[0])):
        out_ref[pl.ds(pl.multiple_of(core * rows, rows), rows), :] = ref[...].astype(
            jnp.float32
        )


def gather_sum(parts, core, cell):
    rows, features = parts[0].shape
    mine = pl.pallas_call(
        put_kernel,
        in_specs=[SMEM] + [VMEM] * 4,
        out_specs=VMEM,
        out_shape=jax.ShapeDtypeStruct((4 * rows, features), parts[0].dtype),
        compiler_params=params(),
        name="put_parts",
    )(cell[None], *parts)
    return pl.pallas_call(
        join_kernel,
        in_specs=[SMEM] + [VMEM] * 2,
        out_specs=VMEM,
        out_shape=jax.ShapeDtypeStruct((8 * rows, features), jnp.float32),
        compiler_params=params(),
        name="join_halves",
    )(core[None], mine, within(mine, 1, 0))


def on_device(inputs, weight, band_vals, far_rows, far_send, far_count, far_vals, grad_out):
    x = inputs[0]
    band = band_vals[0]
    cap = far_send.shape[-1]
    send_index = far_send.reshape(-1)
    target_index = far_rows.reshape(-1)
    count = far_count.reshape(-1)
    vals = far_vals.reshape(-1, BLK, BLK)
    core = lax.axis_index("genome") & 1
    cell = lax.axis_index("cell")

    arrived = exchange(gather_blocks(x, far_send[0, 0].T, far_count[0]))
    low, high = to_neighbours(*rim_terms(x, band))
    band_part = band_sum(x, band)
    output, grads, y, terms = middle(
        cap, target_index, arrived, vals, band_part, low, high, weight, grad_out[0]
    )

    so_far = exchange(terms)
    rims = rim_terms(grads, band)
    rims, y = lax.optimization_barrier((rims, y))
    low, high = to_neighbours(*rims)
    part = scatter_sum(dot_ta(y, grads), core, cell)
    terms = back_terms(1, cap, target_index, grads, vals)
    part, terms = lax.optimization_barrier((part, terms))
    for kind in ("x", "y"):
        sent = part.astype(jnp.bfloat16)
        part = part + sum(shift(sent, kind, s).astype(jnp.float32) for s in (1, 2, 3))
    terms, so_far, part, low, high, grads = lax.optimization_barrier(
        (terms, so_far, part, low, high, grads)
    )

    came_back = exchange(terms)
    so_far = sum_back(0, cap, send_index, count, so_far, band_sum(grads, band), low, high)
    sent = part.astype(jnp.bfloat16)
    grad_weight = gather_sum([sent] + [within(sent, 0, s) for s in (1, 2, 3)], core, cell)
    came_back, so_far, grad_weight = lax.optimization_barrier((came_back, so_far, grad_weight))
    grad_in = tail(1, cap, send_index, count, came_back, so_far, weight.T)
    return (output[None], grad_in[None], grad_weight)


def solution(mesh):
    return jax.shard_map(
        on_device,
        mesh=mesh,
        in_specs=(
            P("cell", "genome", None),
            P(),
            P("cell", "genome", None, None, None),
            P("cell", "genome", None, None),
            P("cell", "genome", None, None),
            P("cell", "genome", None),
            P("cell", "genome", None, None, None, None),
            P("cell", "genome", None),
        ),
        out_specs=(P("cell", "genome", None), P("cell", "genome", None), P()),
        check_vma=False,
    )
```

```python
import functools
import math

import jax
import jax.numpy as jnp
from jax import lax
from jax.experimental import pallas as pl
from jax.experimental.pallas import tpu as pltpu
from jax.sharding import PartitionSpec as P

BLK = 128
BAND = 4
WIDTH = 2 * BAND + 1
CHUNK = 16 * BLK
ROWS_STEP = 256
VMEM_LIMIT = 65_400_000

SMEM = pl.BlockSpec(memory_space=pltpu.SMEM)
VMEM = pl.BlockSpec(memory_space=pltpu.VMEM)
HBM = pl.BlockSpec(memory_space=pltpu.HBM)
ANY = pl.BlockSpec(memory_space=pl.ANY)

band_gain = 3.0
FACTOR = band_gain / math.sqrt(WIDTH * BLK)


def dot(a, b):
    return jnp.dot(a, b, preferred_element_type=jnp.float32)


def dot_ta(a, b):
    return lax.dot_general(a, b, (((0,), (0,)), ((), ())), preferred_element_type=jnp.float32)


def dot_tb(a, b):
    return lax.dot_general(a, b, (((1,), (1,)), ((), ())), preferred_element_type=jnp.float32)


def params():
    return pltpu.CompilerParams(vmem_limit_bytes=VMEM_LIMIT)


def block_rows(index):
    return pl.ds(pl.multiple_of(index * BLK, BLK), BLK)


def gather_kernel(
    index_ref, count_ref, x_ref, out_ref, index, count, x, zeros, small_sems, in_sem, sem
):
    cap, peers = index_ref.shape
    copies = [
        pltpu.make_async_copy(index_ref, index, small_sems.at[0]),
        pltpu.make_async_copy(count_ref, count, small_sems.at[1]),
    ]
    for copy in copies:
        copy.start()
    for i in range(x.shape[0] // ROWS_STEP):
        rows = pl.ds(i * ROWS_STEP, ROWS_STEP)
        pltpu.make_async_copy(x_ref.at[rows], x.at[rows], in_sem).start()
    zeros[...] = jnp.zeros_like(zeros)
    for copy in copies:
        copy.wait()
    pltpu.make_async_copy(x_ref, x, in_sem).wait()

    def send(peer, carry):
        for s in range(cap):
            target = out_ref.at[block_rows(peer * cap + s)]
            live = s < count[0, peer]

            @pl.when(live)
            def _():
                pltpu.make_async_copy(x.at[block_rows(index[s, peer])], target, sem).start()

            @pl.when(jnp.logical_not(live))
            def _():
                pltpu.make_async_copy(zeros, target, sem).start()

        return carry

    lax.fori_loop(0, peers, send, 0)
    pltpu.make_async_copy(out_ref, out_ref, sem).wait()


def gather_blocks(x, index, count):
    cap, peers = index.shape
    features = x.shape[1]
    return pl.pallas_call(
        gather_kernel,
        in_specs=[HBM] * 3,
        out_specs=HBM,
        out_shape=jax.ShapeDtypeStruct((peers * cap * BLK, features), x.dtype),
        scratch_shapes=[
            pltpu.SMEM(index.shape, index.dtype),
            pltpu.SMEM(count.shape, count.dtype),
            pltpu.VMEM(x.shape, x.dtype),
            pltpu.VMEM((BLK, features), x.dtype),
            pltpu.SemaphoreType.DMA((2,)),
            pltpu.SemaphoreType.DMA,
            pltpu.SemaphoreType.DMA,
        ],
        compiler_params=params(),
        cost_estimate=pl.CostEstimate(
            flops=0,
            bytes_accessed=2 * (x.size + peers * cap * BLK * features),
            transcendentals=0,
        ),
        name="gather_blocks",
    )(index, count, x)


def band_kernel(v_ref, band_ref, out_ref, padded, kept, sem):
    step = pl.program_id(0)
    rim = BAND * BLK
    rows, features = v_ref.shape

    @pl.when(step == 0)
    def _():
        padded[pl.ds(0, rim), :] = jnp.zeros((rim, features), padded.dtype)
        padded[pl.ds(rim, rows), :] = v_ref[...]
        padded[pl.ds(rim + rows, rim), :] = jnp.zeros((rim, features), padded.dtype)

    left = jnp.concatenate([band_ref[0, d] for d in range(WIDTH)], axis=1)
    window = padded[pl.ds(pl.multiple_of(step * BLK, BLK), WIDTH * BLK), :]
    rows = block_rows(step)
    kept[rows, :] = FACTOR * dot(left, window)
    pltpu.make_async_copy(kept.at[rows], out_ref.at[rows], sem).start()

    @pl.when(step == pl.num_programs(0) - 1)
    def _():
        pltpu.make_async_copy(kept, out_ref, sem).wait()


def band_sum(v, band):
    rows, features = v.shape
    return pl.pallas_call(
        band_kernel,
        grid=(band.shape[0],),
        in_specs=[
            pl.BlockSpec(v.shape, lambda i: (0, 0)),
            pl.BlockSpec((1, WIDTH, BLK, BLK), lambda i: (i, 0, 0, 0)),
        ],
        out_specs=ANY,
        out_shape=jax.ShapeDtypeStruct((rows, features), jnp.float32),
        scratch_shapes=[
            pltpu.VMEM((rows + 2 * BAND * BLK, features), v.dtype),
            pltpu.VMEM((rows, features), jnp.float32),
            pltpu.SemaphoreType.DMA,
        ],
        compiler_params=params(),
        cost_estimate=pl.CostEstimate(
            flops=17 * 2 * band.size * features,
            bytes_accessed=17 * (2 * band.size + 6 * v.size),
            transcendentals=0,
        ),
        name="band_sum",
    )(v, band)


def rim_kernel(v_ref, first_ref, last_ref, low_ref, high_ref):
    start = v_ref.shape[0] - BAND * BLK
    for m in range(BAND):
        rows = pl.ds(m * BLK, BLK)
        left = jnp.concatenate([first_ref[j, m - j] for j in range(m + 1)], axis=0)
        term = dot_ta(left, v_ref[pl.ds(0, (m + 1) * BLK), :])
        low_ref[rows, :] = (FACTOR * term).astype(low_ref.dtype)
        left = jnp.concatenate([last_ref[j, 2 * BAND + m - j] for j in range(m, BAND)], axis=0)
        term = dot_ta(left, v_ref[pl.ds(start + m * BLK, (BAND - m) * BLK), :])
        high_ref[rows, :] = (FACTOR * term).astype(high_ref.dtype)


def rim_terms(v, band):
    blocks = band.shape[0]
    features = v.shape[1]
    part = (BAND,) + band.shape[1:]
    out = jax.ShapeDtypeStruct((BAND * BLK, features), v.dtype)
    return pl.pallas_call(
        rim_kernel,
        grid=(1,),
        in_specs=[
            pl.BlockSpec(v.shape, lambda i: (0, 0)),
            pl.BlockSpec(part, lambda i: (0, 0, 0, 0)),
            pl.BlockSpec(part, lambda i: (blocks // BAND - 1, 0, 0, 0)),
        ],
        out_specs=[pl.BlockSpec(out.shape, lambda i: (0, 0))] * 2,
        out_shape=[out] * 2,
        compiler_params=params(),
        cost_estimate=pl.CostEstimate(
            flops=2 * 20 * BLK * BLK * features, bytes_accessed=6 << 20, transcendentals=0
        ),
        name="rim_terms",
    )(v, band, band)


def to_neighbours(low, high):
    count = lax.axis_size("genome")
    forward = [(i, i + 1) for i in range(count - 1)]
    backward = [(target, source) for source, target in forward]
    return lax.ppermute(high, "genome", forward), lax.ppermute(low, "genome", backward)


def fetches(sources, targets, sems):
    copies = [
        pltpu.make_async_copy(source, target, sems.at[k])
        for k, (source, target) in enumerate(zip(sources, targets))
    ]
    for copy in copies:
        copy.start()
    return copies


def chunk_copy(source, target, sems, i):
    rows = pl.ds(i * CHUNK, CHUNK)
    return pltpu.make_async_copy(source.at[rows], target.at[rows], sems.at[i])


def send_terms(s, cap, target_ref, grads, vals, blocks, terms_ref, sem):
    peers = terms_ref.shape[0] // BLK
    group = CHUNK // BLK

    def chunk(i, carry):
        for j in range(group):
            peer = i * group + j
            slot = peer * cap + s
            term = dot_ta(vals[slot], grads[block_rows(target_ref[slot]), :])
            blocks[block_rows(peer), :] = term.astype(jnp.bfloat16)
            if j % 4 == 3:
                rows = pl.ds(pl.multiple_of((peer - 3) * BLK, 4 * BLK), 4 * BLK)
                pltpu.make_async_copy(blocks.at[rows], terms_ref.at[rows], sem).start()
        return carry

    lax.fori_loop(0, peers // group, chunk, 0)


def middle_kernel(
    cap,
    target_ref,
    arrived_ref,
    vals_ref,
    band_ref,
    low_ref,
    high_ref,
    weight_ref,
    grad_ref,
    output_ref,
    grads_ref,
    y_ref,
    terms_ref,
    blocks,
    vals,
    total,
    low,
    high,
    weight,
    grad,
    kept,
    block_sems,
    sems,
    out_sems,
):
    chunks = blocks.shape[0] // CHUNK
    slots = CHUNK // BLK
    count = total.shape[0]
    steps = count // ROWS_STEP
    rim = low.shape[0]
    first = fetches((band_ref, vals_ref), (total, vals), sems)
    for i in range(chunks):
        chunk_copy(arrived_ref, blocks, block_sems, i).start()
    later = fetches(
        (low_ref, high_ref, weight_ref, grad_ref), (low, high, weight, grad), sems.at[pl.ds(2, 4)]
    )
    for copy in first:
        copy.wait()

    def add_chunk(i, carry):
        rows = pl.ds(pl.multiple_of(i * CHUNK, CHUNK), CHUNK)
        pltpu.make_async_copy(arrived_ref.at[rows], blocks.at[rows], block_sems.at[i]).wait()
        for j in range(slots):
            slot = i * slots + j
            rows = block_rows(target_ref[slot])
            total[rows, :] += dot(vals[slot], blocks[block_rows(slot), :])
        return carry

    lax.fori_loop(0, chunks, add_chunk, 0)
    for copy in later:
        copy.wait()

    outs = (output_ref, grads_ref, y_ref)
    for i in range(steps):
        start = i * ROWS_STEP
        rows = pl.ds(start, ROWS_STEP)
        summed = total[rows, :]
        if start < rim:
            summed = summed + low[rows, :].astype(jnp.float32)
        if start >= count - rim:
            edge = pl.ds(start - (count - rim), ROWS_STEP)
            summed = summed + high[edge, :].astype(jnp.float32)
        y = summed.astype(jnp.bfloat16)
        kept[2, rows, :] = y
        preact = dot(y, weight[...])
        sigma = jax.nn.sigmoid(preact)
        kept[0, rows, :] = (preact * sigma).astype(jnp.bfloat16)
        slope = sigma * (1.0 + preact * (1.0 - sigma))
        kept[1, rows, :] = (grad[rows, :].astype(jnp.float32) * slope).astype(jnp.bfloat16)
        for k in range(3):
            pltpu.make_async_copy(kept.at[k, rows], outs[k].at[rows], out_sems.at[k]).start()

    send_terms(0, cap, target_ref, kept.at[1], vals, blocks, terms_ref, out_sems.at[3])
    for k in range(3):
        pltpu.make_async_copy(kept.at[k], outs[k], out_sems.at[k]).wait()
    pltpu.make_async_copy(terms_ref, terms_ref, out_sems.at[3]).wait()


def middle(cap, target, arrived, vals, band, low, high, weight, grad_out):
    rows, features = grad_out.shape
    out = jax.ShapeDtypeStruct((rows, features), jnp.bfloat16)
    same = lambda v: pltpu.VMEM(v.shape, v.dtype)
    return pl.pallas_call(
        functools.partial(middle_kernel, cap),
        in_specs=[SMEM] + [HBM] * 3 + [ANY] * 2 + [HBM] * 2,
        out_specs=[HBM] * 4,
        out_shape=[out] * 3 + [jax.ShapeDtypeStruct((arrived.shape[0] // cap, features), jnp.bfloat16)],
        scratch_shapes=[
            *(same(v) for v in (arrived, vals, band, low, high, weight, grad_out)),
            pltpu.VMEM((3, rows, features), jnp.bfloat16),
            pltpu.SemaphoreType.DMA((arrived.shape[0] // CHUNK,)),
            pltpu.SemaphoreType.DMA((6,)),
            pltpu.SemaphoreType.DMA((4,)),
        ],
        compiler_params=params(),
        cost_estimate=pl.CostEstimate(
            flops=2 * (2 * vals.size + rows * features) * features,
            bytes_accessed=2 * (2 * arrived.size + vals.size + 6 * rows * features),
            transcendentals=rows * features,
        ),
        name="middle",
    )(target, arrived, vals, band, low, high, weight, grad_out)


def back_kernel(s, cap, target_ref, grads_ref, vals_ref, terms_ref, grads, vals, blocks, sems, sem):
    for copy in fetches((grads_ref, vals_ref), (grads, vals), sems):
        copy.wait()
    send_terms(s, cap, target_ref, grads, vals, blocks, terms_ref, sem)
    pltpu.make_async_copy(blocks, terms_ref, sem).wait()


def back_terms(s, cap, target, grads, vals):
    shape = (vals.shape[0] // cap * BLK, grads.shape[1])
    return pl.pallas_call(
        functools.partial(back_kernel, s, cap),
        in_specs=[SMEM, HBM, HBM],
        out_specs=HBM,
        out_shape=jax.ShapeDtypeStruct(shape, jnp.bfloat16),
        scratch_shapes=[
            pltpu.VMEM(grads.shape, grads.dtype),
            pltpu.VMEM(vals.shape, vals.dtype),
            pltpu.VMEM(shape, jnp.bfloat16),
            pltpu.SemaphoreType.DMA((2,)),
            pltpu.SemaphoreType.DMA,
        ],
        compiler_params=params(),
        cost_estimate=pl.CostEstimate(
            flops=2 * vals.size * shape[1] // cap, bytes_accessed=8 << 20, transcendentals=0
        ),
        name="back_terms",
    )(target, grads, vals)


def add_back(s, cap, index_ref, count_ref, back_ref, back, sems, total):
    group = CHUNK // BLK

    def chunk(i, carry):
        rows = pl.ds(pl.multiple_of(i * CHUNK, CHUNK), CHUNK)
        pltpu.make_async_copy(back_ref.at[rows], back.at[rows], sems.at[i]).wait()
        for j in range(group):
            peer = i * group + j

            @pl.when(s < count_ref[peer])
            def _():
                rows = block_rows(index_ref[peer * cap + s])
                total[rows, :] += back[block_rows(peer), :].astype(jnp.float32)

        return carry

    lax.fori_loop(0, back.shape[0] // CHUNK, chunk, 0)


def sum_kernel(
    s,
    cap,
    index_ref,
    count_ref,
    back_ref,
    band_ref,
    low_ref,
    high_ref,
    out_ref,
    back,
    total,
    low,
    high,
    sems,
    sem,
):
    rim = low.shape[0]
    first = fetches((band_ref, low_ref, high_ref), (total, low, high), sem)
    for i in range(back.shape[0] // CHUNK):
        chunk_copy(back_ref, back, sems, i).start()
    for copy in first:
        copy.wait()
    total[pl.ds(0, rim), :] += low[...].astype(jnp.float32)
    total[pl.ds(total.shape[0] - rim, rim), :] += high[...].astype(jnp.float32)
    add_back(s, cap, index_ref, count_ref, back_ref, back, sems, total)
    out = pltpu.make_async_copy(total, out_ref, sem.at[0])
    out.start()
    out.wait()


def sum_back(s, cap, index, count, back, band, low, high):
    return pl.pallas_call(
        functools.partial(sum_kernel, s, cap),
        in_specs=[SMEM] * 2 + [HBM] * 2 + [ANY] * 2,
        out_specs=HBM,
        out_shape=jax.ShapeDtypeStruct(band.shape, jnp.float32),
        scratch_shapes=[
            *(pltpu.VMEM(v.shape, v.dtype) for v in (back, band, low, high)),
            pltpu.SemaphoreType.DMA((back.shape[0] // CHUNK,)),
            pltpu.SemaphoreType.DMA((3,)),
        ],
        compiler_params=params(),
        cost_estimate=pl.CostEstimate(
            flops=band.size, bytes_accessed=12 << 20, transcendentals=0
        ),
        name="sum_back",
    )(index, count, back, band, low, high)


def tail_kernel(
    s,
    cap,
    index_ref,
    count_ref,
    back_ref,
    sum_ref,
    weight_ref,
    out_ref,
    back,
    total,
    weight,
    kept,
    back_sems,
    sems,
    sem,
):
    first = fetches((sum_ref,), (total,), sems)
    for i in range(back.shape[0] // CHUNK):
        chunk_copy(back_ref, back, back_sems, i).start()
    later = fetches((weight_ref,), (weight,), sems.at[pl.ds(1, 1)])
    for copy in first:
        copy.wait()
    add_back(s, cap, index_ref, count_ref, back_ref, back, back_sems, total)
    for copy in later:
        copy.wait()
    for i in range(total.shape[0] // ROWS_STEP):
        rows = pl.ds(i * ROWS_STEP, ROWS_STEP)
        grad_z = total[rows, :].astype(jnp.bfloat16)
        kept[rows, :] = dot(grad_z, weight[...]).astype(jnp.bfloat16)
        pltpu.make_async_copy(kept.at[rows], out_ref.at[rows], sem).start()
    pltpu.make_async_copy(kept, out_ref, sem).wait()


def tail(s, cap, index, count, back, so_far, weight_t):
    same = lambda v: pltpu.VMEM(v.shape, v.dtype)
    return pl.pallas_call(
        functools.partial(tail_kernel, s, cap),
        in_specs=[SMEM] * 2 + [HBM] * 3,
        out_specs=HBM,
        out_shape=jax.ShapeDtypeStruct(so_far.shape, jnp.bfloat16),
        scratch_shapes=[
            *(same(v) for v in (back, so_far, weight_t)),
            pltpu.VMEM(so_far.shape, jnp.bfloat16),
            pltpu.SemaphoreType.DMA((back.shape[0] // CHUNK,)),
            pltpu.SemaphoreType.DMA((2,)),
            pltpu.SemaphoreType.DMA,
        ],
        compiler_params=params(),
        cost_estimate=pl.CostEstimate(
            flops=2 * so_far.size * weight_t.shape[1],
            bytes_accessed=2 * back.size + 6 * so_far.size,
            transcendentals=0,
        ),
        name="tail",
    )(index, count, back, so_far, weight_t)


def exchange(blocks):
    peers = lax.axis_size("genome")
    cut = blocks.reshape(peers, -1, blocks.shape[-1])
    return lax.all_to_all(cut, "genome", 0, 0, tiled=True).reshape(blocks.shape)


def moved(index, kind, s):
    core, x, y = index & 1, (index >> 1) & 3, index >> 3
    if kind == "x":
        x = (x + s) & 3
    else:
        y = (y + s) & 3
    return y * 8 + x * 2 + core


def shift(v, kind, s):
    return lax.ppermute(v, "genome", [(i, moved(i, kind, s)) for i in range(32)])


def within(v, flip, s):
    pairs = [
        (g * 4 + c, (g ^ flip) * 4 + ((c + s) & 3)) for g in range(32) for c in range(4)
    ]
    return lax.ppermute(v, ("genome", "cell"), pairs)


def scatter_sum(v, core, cell):
    rows = v.shape[0] // 8
    total = None
    for flip in (0, 1):
        for s in range(4):
            owner = (core ^ flip) * 4 + ((cell + s) & 3)
            part = lax.dynamic_slice_in_dim(v, owner * rows, rows, axis=0)
            part = part if (flip, s) == (0, 0) else within(part, flip, s)
            total = part if total is None else total + part
    return total


def put_kernel(cell_ref, *refs):
    out_ref = refs[-1]
    rows = refs[0].shape[0]
    for s, ref in enumerate(refs[:-1]):
        place = ((cell_ref[0] - s) & 3) * rows
        out_ref[pl.ds(pl.multiple_of(place, rows), rows), :] = ref[...]


def join_kernel(core_ref, mine_ref, other_ref, out_ref):
    rows = mine_ref.shape[0]
    for ref, core in ((mine_ref, core_ref[0]), (other_ref, 1 - core_ref[0])):
        out_ref[pl.ds(pl.multiple_of(core * rows, rows), rows), :] = ref[...].astype(
            jnp.float32
        )


def gather_sum(parts, core, cell):
    rows, features = parts[0].shape
    mine = pl.pallas_call(
        put_kernel,
        in_specs=[SMEM] + [VMEM] * 4,
        out_specs=VMEM,
        out_shape=jax.ShapeDtypeStruct((4 * rows, features), parts[0].dtype),
        compiler_params=params(),
        name="put_parts",
    )(cell[None], *parts)
    return pl.pallas_call(
        join_kernel,
        in_specs=[SMEM] + [VMEM] * 2,
        out_specs=VMEM,
        out_shape=jax.ShapeDtypeStruct((8 * rows, features), jnp.float32),
        compiler_params=params(),
        name="join_halves",
    )(core[None], mine, within(mine, 1, 0))


def on_device(inputs, weight, band_vals, far_rows, far_send, far_count, far_vals, grad_out):
    x = inputs[0]
    band = band_vals[0]
    cap = far_send.shape[-1]
    send_index = far_send.reshape(-1)
    target_index = far_rows.reshape(-1)
    count = far_count.reshape(-1)
    vals = far_vals.reshape(-1, BLK, BLK)
    core = lax.axis_index("genome") & 1
    cell = lax.axis_index("cell")

    arrived = exchange(gather_blocks(x, far_send[0, 0].T, far_count[0]))
    low, high = to_neighbours(*rim_terms(x, band))
    band_part = band_sum(x, band)
    output, grads, y, terms = middle(
        cap, target_index, arrived, vals, band_part, low, high, weight, grad_out[0]
    )

    so_far = exchange(terms)
    rims = rim_terms(grads, band)
    rims, y = lax.optimization_barrier((rims, y))
    low, high = to_neighbours(*rims)
    part = scatter_sum(dot_ta(y, grads), core, cell)
    terms = back_terms(1, cap, target_index, grads, vals)
    part, terms = lax.optimization_barrier((part, terms))
    sent = part.astype(jnp.bfloat16)
    part = part + sum(shift(sent, "x", s).astype(jnp.float32) for s in (1, 2, 3))
    terms, so_far, part, low, high, grads = lax.optimization_barrier(
        (terms, so_far, part, low, high, grads)
    )

    came_back = exchange(terms)
    so_far = sum_back(0, cap, send_index, count, so_far, band_sum(grads, band), low, high)
    sent = part.astype(jnp.bfloat16)
    part = part + sum(shift(sent, "y", s).astype(jnp.float32) for s in (1, 2, 3))
    sent = part.astype(jnp.bfloat16)
    grad_weight = gather_sum([sent] + [within(sent, 0, s) for s in (1, 2, 3)], core, cell)
    came_back, so_far, grad_weight = lax.optimization_barrier((came_back, so_far, grad_weight))
    grad_in = tail(1, cap, send_index, count, came_back, so_far, weight.T)
    return (output[None], grad_in[None], grad_weight)


def solution(mesh):
    return jax.shard_map(
        on_device,
        mesh=mesh,
        in_specs=(
            P("cell", "genome", None),
            P(),
            P("cell", "genome", None, None, None),
            P("cell", "genome", None, None),
            P("cell", "genome", None, None),
            P("cell", "genome", None),
            P("cell", "genome", None, None, None, None),
            P("cell", "genome", None),
        ),
        out_specs=(P("cell", "genome", None), P("cell", "genome", None), P()),
        check_vma=False,
    )
```

```python
import functools
import math

import jax
import jax.numpy as jnp
from jax import lax
from jax.experimental import pallas as pl
from jax.experimental.pallas import tpu as pltpu
from jax.sharding import PartitionSpec as P

BLK = 128
BAND = 4
WIDTH = 2 * BAND + 1
CHUNK = 16 * BLK
ROWS_STEP = 256
VMEM_LIMIT = 65_400_000

SMEM = pl.BlockSpec(memory_space=pltpu.SMEM)
VMEM = pl.BlockSpec(memory_space=pltpu.VMEM)
HBM = pl.BlockSpec(memory_space=pltpu.HBM)
ANY = pl.BlockSpec(memory_space=pl.ANY)

band_gain = 3.0
FACTOR = band_gain / math.sqrt(WIDTH * BLK)


def dot(a, b):
    return jnp.dot(a, b, preferred_element_type=jnp.float32)


def dot_ta(a, b):
    return lax.dot_general(a, b, (((0,), (0,)), ((), ())), preferred_element_type=jnp.float32)


def dot_tb(a, b):
    return lax.dot_general(a, b, (((1,), (1,)), ((), ())), preferred_element_type=jnp.float32)


def params():
    return pltpu.CompilerParams(vmem_limit_bytes=VMEM_LIMIT)


def block_rows(index):
    return pl.ds(pl.multiple_of(index * BLK, BLK), BLK)


def gather_kernel(
    index_ref, count_ref, x_ref, out_ref, index, count, x, zeros, small_sems, in_sem, sem
):
    cap, peers = index_ref.shape
    copies = [
        pltpu.make_async_copy(index_ref, index, small_sems.at[0]),
        pltpu.make_async_copy(count_ref, count, small_sems.at[1]),
    ]
    for copy in copies:
        copy.start()
    for i in range(x.shape[0] // ROWS_STEP):
        rows = pl.ds(i * ROWS_STEP, ROWS_STEP)
        pltpu.make_async_copy(x_ref.at[rows], x.at[rows], in_sem).start()
    zeros[...] = jnp.zeros_like(zeros)
    for copy in copies:
        copy.wait()
    pltpu.make_async_copy(x_ref, x, in_sem).wait()

    def send(peer, carry):
        for s in range(cap):
            target = out_ref.at[block_rows(peer * cap + s)]
            live = s < count[0, peer]

            @pl.when(live)
            def _():
                pltpu.make_async_copy(x.at[block_rows(index[s, peer])], target, sem).start()

            @pl.when(jnp.logical_not(live))
            def _():
                pltpu.make_async_copy(zeros, target, sem).start()

        return carry

    lax.fori_loop(0, peers, send, 0)
    pltpu.make_async_copy(out_ref, out_ref, sem).wait()


def gather_blocks(x, index, count):
    cap, peers = index.shape
    features = x.shape[1]
    return pl.pallas_call(
        gather_kernel,
        in_specs=[HBM] * 3,
        out_specs=HBM,
        out_shape=jax.ShapeDtypeStruct((peers * cap * BLK, features), x.dtype),
        scratch_shapes=[
            pltpu.SMEM(index.shape, index.dtype),
            pltpu.SMEM(count.shape, count.dtype),
            pltpu.VMEM(x.shape, x.dtype),
            pltpu.VMEM((BLK, features), x.dtype),
            pltpu.SemaphoreType.DMA((2,)),
            pltpu.SemaphoreType.DMA,
            pltpu.SemaphoreType.DMA,
        ],
        compiler_params=params(),
        cost_estimate=pl.CostEstimate(
            flops=0,
            bytes_accessed=2 * (x.size + peers * cap * BLK * features),
            transcendentals=0,
        ),
        name="gather_blocks",
    )(index, count, x)


def band_kernel(v_ref, band_ref, out_ref, padded, kept, sem):
    step = pl.program_id(0)
    rim = BAND * BLK
    rows, features = v_ref.shape

    @pl.when(step == 0)
    def _():
        padded[pl.ds(0, rim), :] = jnp.zeros((rim, features), padded.dtype)
        padded[pl.ds(rim, rows), :] = v_ref[...]
        padded[pl.ds(rim + rows, rim), :] = jnp.zeros((rim, features), padded.dtype)

    left = jnp.concatenate([band_ref[0, d] for d in range(WIDTH)], axis=1)
    window = padded[pl.ds(pl.multiple_of(step * BLK, BLK), WIDTH * BLK), :]
    rows = block_rows(step)
    kept[rows, :] = FACTOR * dot(left, window)
    pltpu.make_async_copy(kept.at[rows], out_ref.at[rows], sem).start()

    @pl.when(step == pl.num_programs(0) - 1)
    def _():
        pltpu.make_async_copy(kept, out_ref, sem).wait()


def band_sum(v, band):
    rows, features = v.shape
    return pl.pallas_call(
        band_kernel,
        grid=(band.shape[0],),
        in_specs=[
            pl.BlockSpec(v.shape, lambda i: (0, 0)),
            pl.BlockSpec((1, WIDTH, BLK, BLK), lambda i: (i, 0, 0, 0)),
        ],
        out_specs=ANY,
        out_shape=jax.ShapeDtypeStruct((rows, features), jnp.float32),
        scratch_shapes=[
            pltpu.VMEM((rows + 2 * BAND * BLK, features), v.dtype),
            pltpu.VMEM((rows, features), jnp.float32),
            pltpu.SemaphoreType.DMA,
        ],
        compiler_params=params(),
        cost_estimate=pl.CostEstimate(
            flops=17 * 2 * band.size * features,
            bytes_accessed=17 * (2 * band.size + 6 * v.size),
            transcendentals=0,
        ),
        name="band_sum",
    )(v, band)


def rim_kernel(v_ref, first_ref, last_ref, low_ref, high_ref):
    start = v_ref.shape[0] - BAND * BLK
    for m in range(BAND):
        rows = pl.ds(m * BLK, BLK)
        left = jnp.concatenate([first_ref[j, m - j] for j in range(m + 1)], axis=0)
        term = dot_ta(left, v_ref[pl.ds(0, (m + 1) * BLK), :])
        low_ref[rows, :] = (FACTOR * term).astype(low_ref.dtype)
        left = jnp.concatenate([last_ref[j, 2 * BAND + m - j] for j in range(m, BAND)], axis=0)
        term = dot_ta(left, v_ref[pl.ds(start + m * BLK, (BAND - m) * BLK), :])
        high_ref[rows, :] = (FACTOR * term).astype(high_ref.dtype)


def rim_terms(v, band):
    blocks = band.shape[0]
    features = v.shape[1]
    part = (BAND,) + band.shape[1:]
    out = jax.ShapeDtypeStruct((BAND * BLK, features), v.dtype)
    return pl.pallas_call(
        rim_kernel,
        grid=(1,),
        in_specs=[
            pl.BlockSpec(v.shape, lambda i: (0, 0)),
            pl.BlockSpec(part, lambda i: (0, 0, 0, 0)),
            pl.BlockSpec(part, lambda i: (blocks // BAND - 1, 0, 0, 0)),
        ],
        out_specs=[pl.BlockSpec(out.shape, lambda i: (0, 0))] * 2,
        out_shape=[out] * 2,
        compiler_params=params(),
        cost_estimate=pl.CostEstimate(
            flops=2 * 20 * BLK * BLK * features, bytes_accessed=6 << 20, transcendentals=0
        ),
        name="rim_terms",
    )(v, band, band)


def to_neighbours(low, high):
    count = lax.axis_size("genome")
    forward = [(i, i + 1) for i in range(count - 1)]
    backward = [(target, source) for source, target in forward]
    return lax.ppermute(high, "genome", forward), lax.ppermute(low, "genome", backward)


def fetches(sources, targets, sems):
    copies = [
        pltpu.make_async_copy(source, target, sems.at[k])
        for k, (source, target) in enumerate(zip(sources, targets))
    ]
    for copy in copies:
        copy.start()
    return copies


def chunk_copy(source, target, sems, i):
    rows = pl.ds(i * CHUNK, CHUNK)
    return pltpu.make_async_copy(source.at[rows], target.at[rows], sems.at[i])


def send_terms(s, cap, target_ref, grads, vals, blocks, terms_ref, sem):
    peers = terms_ref.shape[0] // BLK
    group = CHUNK // BLK

    def chunk(i, carry):
        for j in range(group):
            peer = i * group + j
            slot = peer * cap + s
            term = dot_ta(vals[slot], grads[block_rows(target_ref[slot]), :])
            blocks[block_rows(peer), :] = term.astype(jnp.bfloat16)
            if j % 4 == 3:
                rows = pl.ds(pl.multiple_of((peer - 3) * BLK, 4 * BLK), 4 * BLK)
                pltpu.make_async_copy(blocks.at[rows], terms_ref.at[rows], sem).start()
        return carry

    lax.fori_loop(0, peers // group, chunk, 0)


def middle_kernel(
    cap,
    target_ref,
    arrived_ref,
    vals_ref,
    band_ref,
    low_ref,
    high_ref,
    weight_ref,
    grad_ref,
    output_ref,
    grads_ref,
    y_ref,
    terms_ref,
    blocks,
    vals,
    total,
    low,
    high,
    weight,
    grad,
    kept,
    block_sems,
    sems,
    out_sems,
):
    chunks = blocks.shape[0] // CHUNK
    slots = CHUNK // BLK
    count = total.shape[0]
    steps = count // ROWS_STEP
    rim = low.shape[0]
    first = fetches((band_ref, vals_ref), (total, vals), sems)
    for i in range(chunks):
        chunk_copy(arrived_ref, blocks, block_sems, i).start()
    later = fetches(
        (low_ref, high_ref, weight_ref, grad_ref), (low, high, weight, grad), sems.at[pl.ds(2, 4)]
    )
    for copy in first:
        copy.wait()

    def add_chunk(i, carry):
        rows = pl.ds(pl.multiple_of(i * CHUNK, CHUNK), CHUNK)
        pltpu.make_async_copy(arrived_ref.at[rows], blocks.at[rows], block_sems.at[i]).wait()
        for j in range(slots):
            slot = i * slots + j
            rows = block_rows(target_ref[slot])
            total[rows, :] += dot(vals[slot], blocks[block_rows(slot), :])
        return carry

    lax.fori_loop(0, chunks, add_chunk, 0)
    for copy in later:
        copy.wait()

    outs = (output_ref, grads_ref, y_ref)
    for i in range(steps):
        start = i * ROWS_STEP
        rows = pl.ds(start, ROWS_STEP)
        summed = total[rows, :]
        if start < rim:
            summed = summed + low[rows, :].astype(jnp.float32)
        if start >= count - rim:
            edge = pl.ds(start - (count - rim), ROWS_STEP)
            summed = summed + high[edge, :].astype(jnp.float32)
        y = summed.astype(jnp.bfloat16)
        kept[2, rows, :] = y
        preact = dot(y, weight[...])
        sigma = jax.nn.sigmoid(preact)
        kept[0, rows, :] = (preact * sigma).astype(jnp.bfloat16)
        slope = sigma * (1.0 + preact * (1.0 - sigma))
        kept[1, rows, :] = (grad[rows, :].astype(jnp.float32) * slope).astype(jnp.bfloat16)
        for k in range(3):
            pltpu.make_async_copy(kept.at[k, rows], outs[k].at[rows], out_sems.at[k]).start()

    send_terms(0, cap, target_ref, kept.at[1], vals, blocks, terms_ref, out_sems.at[3])
    for k in range(3):
        pltpu.make_async_copy(kept.at[k], outs[k], out_sems.at[k]).wait()
    pltpu.make_async_copy(terms_ref, terms_ref, out_sems.at[3]).wait()


def middle(cap, target, arrived, vals, band, low, high, weight, grad_out):
    rows, features = grad_out.shape
    out = jax.ShapeDtypeStruct((rows, features), jnp.bfloat16)
    same = lambda v: pltpu.VMEM(v.shape, v.dtype)
    return pl.pallas_call(
        functools.partial(middle_kernel, cap),
        in_specs=[SMEM] + [HBM] * 3 + [ANY] * 2 + [HBM] * 2,
        out_specs=[HBM] * 4,
        out_shape=[out] * 3 + [jax.ShapeDtypeStruct((arrived.shape[0] // cap, features), jnp.bfloat16)],
        scratch_shapes=[
            *(same(v) for v in (arrived, vals, band, low, high, weight, grad_out)),
            pltpu.VMEM((3, rows, features), jnp.bfloat16),
            pltpu.SemaphoreType.DMA((arrived.shape[0] // CHUNK,)),
            pltpu.SemaphoreType.DMA((6,)),
            pltpu.SemaphoreType.DMA((4,)),
        ],
        compiler_params=params(),
        cost_estimate=pl.CostEstimate(
            flops=2 * (2 * vals.size + rows * features) * features,
            bytes_accessed=2 * (2 * arrived.size + vals.size + 6 * rows * features),
            transcendentals=rows * features,
        ),
        name="middle",
    )(target, arrived, vals, band, low, high, weight, grad_out)


def back_kernel(s, cap, target_ref, grads_ref, vals_ref, terms_ref, grads, vals, blocks, sems, sem):
    for copy in fetches((grads_ref, vals_ref), (grads, vals), sems):
        copy.wait()
    send_terms(s, cap, target_ref, grads, vals, blocks, terms_ref, sem)
    pltpu.make_async_copy(blocks, terms_ref, sem).wait()


def back_terms(s, cap, target, grads, vals):
    shape = (vals.shape[0] // cap * BLK, grads.shape[1])
    return pl.pallas_call(
        functools.partial(back_kernel, s, cap),
        in_specs=[SMEM, HBM, HBM],
        out_specs=HBM,
        out_shape=jax.ShapeDtypeStruct(shape, jnp.bfloat16),
        scratch_shapes=[
            pltpu.VMEM(grads.shape, grads.dtype),
            pltpu.VMEM(vals.shape, vals.dtype),
            pltpu.VMEM(shape, jnp.bfloat16),
            pltpu.SemaphoreType.DMA((2,)),
            pltpu.SemaphoreType.DMA,
        ],
        compiler_params=params(),
        cost_estimate=pl.CostEstimate(
            flops=2 * vals.size * shape[1] // cap, bytes_accessed=8 << 20, transcendentals=0
        ),
        name="back_terms",
    )(target, grads, vals)


def add_back(s, cap, index_ref, count_ref, back_ref, back, sems, total):
    group = CHUNK // BLK

    def chunk(i, carry):
        rows = pl.ds(pl.multiple_of(i * CHUNK, CHUNK), CHUNK)
        pltpu.make_async_copy(back_ref.at[rows], back.at[rows], sems.at[i]).wait()
        for j in range(group):
            peer = i * group + j

            @pl.when(s < count_ref[peer])
            def _():
                rows = block_rows(index_ref[peer * cap + s])
                total[rows, :] += back[block_rows(peer), :].astype(jnp.float32)

        return carry

    lax.fori_loop(0, back.shape[0] // CHUNK, chunk, 0)


def sum_kernel(
    s,
    cap,
    index_ref,
    count_ref,
    back_ref,
    band_ref,
    low_ref,
    high_ref,
    out_ref,
    back,
    total,
    low,
    high,
    sems,
    sem,
):
    rim = low.shape[0]
    first = fetches((band_ref, low_ref, high_ref), (total, low, high), sem)
    for i in range(back.shape[0] // CHUNK):
        chunk_copy(back_ref, back, sems, i).start()
    for copy in first:
        copy.wait()
    total[pl.ds(0, rim), :] += low[...].astype(jnp.float32)
    total[pl.ds(total.shape[0] - rim, rim), :] += high[...].astype(jnp.float32)
    add_back(s, cap, index_ref, count_ref, back_ref, back, sems, total)
    out = pltpu.make_async_copy(total, out_ref, sem.at[0])
    out.start()
    out.wait()


def sum_back(s, cap, index, count, back, band, low, high):
    return pl.pallas_call(
        functools.partial(sum_kernel, s, cap),
        in_specs=[SMEM] * 2 + [HBM] * 2 + [ANY] * 2,
        out_specs=HBM,
        out_shape=jax.ShapeDtypeStruct(band.shape, jnp.float32),
        scratch_shapes=[
            *(pltpu.VMEM(v.shape, v.dtype) for v in (back, band, low, high)),
            pltpu.SemaphoreType.DMA((back.shape[0] // CHUNK,)),
            pltpu.SemaphoreType.DMA((3,)),
        ],
        compiler_params=params(),
        cost_estimate=pl.CostEstimate(
            flops=band.size, bytes_accessed=12 << 20, transcendentals=0
        ),
        name="sum_back",
    )(index, count, back, band, low, high)


def tail_kernel(
    s,
    cap,
    index_ref,
    count_ref,
    back_ref,
    sum_ref,
    weight_ref,
    out_ref,
    back,
    total,
    weight,
    kept,
    back_sems,
    sems,
    sem,
):
    first = fetches((sum_ref,), (total,), sems)
    for i in range(back.shape[0] // CHUNK):
        chunk_copy(back_ref, back, back_sems, i).start()
    later = fetches((weight_ref,), (weight,), sems.at[pl.ds(1, 1)])
    for copy in first:
        copy.wait()
    add_back(s, cap, index_ref, count_ref, back_ref, back, back_sems, total)
    for copy in later:
        copy.wait()
    for i in range(total.shape[0] // ROWS_STEP):
        rows = pl.ds(i * ROWS_STEP, ROWS_STEP)
        grad_z = total[rows, :].astype(jnp.bfloat16)
        kept[rows, :] = dot(grad_z, weight[...]).astype(jnp.bfloat16)
        pltpu.make_async_copy(kept.at[rows], out_ref.at[rows], sem).start()
    pltpu.make_async_copy(kept, out_ref, sem).wait()


def tail(s, cap, index, count, back, so_far, weight_t):
    same = lambda v: pltpu.VMEM(v.shape, v.dtype)
    return pl.pallas_call(
        functools.partial(tail_kernel, s, cap),
        in_specs=[SMEM] * 2 + [HBM] * 3,
        out_specs=HBM,
        out_shape=jax.ShapeDtypeStruct(so_far.shape, jnp.bfloat16),
        scratch_shapes=[
            *(same(v) for v in (back, so_far, weight_t)),
            pltpu.VMEM(so_far.shape, jnp.bfloat16),
            pltpu.SemaphoreType.DMA((back.shape[0] // CHUNK,)),
            pltpu.SemaphoreType.DMA((2,)),
            pltpu.SemaphoreType.DMA,
        ],
        compiler_params=params(),
        cost_estimate=pl.CostEstimate(
            flops=2 * so_far.size * weight_t.shape[1],
            bytes_accessed=2 * back.size + 6 * so_far.size,
            transcendentals=0,
        ),
        name="tail",
    )(index, count, back, so_far, weight_t)


def exchange(blocks):
    peers = lax.axis_size("genome")
    cut = blocks.reshape(peers, -1, blocks.shape[-1])
    return lax.all_to_all(cut, "genome", 0, 0, tiled=True).reshape(blocks.shape)


def moved(index, kind, s):
    core, x, y = index & 1, (index >> 1) & 3, index >> 3
    if kind == "x":
        x = (x + s) & 3
    else:
        y = (y + s) & 3
    return y * 8 + x * 2 + core


def shift(v, kind, s):
    return lax.ppermute(v, "genome", [(i, moved(i, kind, s)) for i in range(32)])


def within(v, flip, s):
    pairs = [
        (g * 4 + c, (g ^ flip) * 4 + ((c + s) & 3)) for g in range(32) for c in range(4)
    ]
    return lax.ppermute(v, ("genome", "cell"), pairs)


def scatter_sum(v, core, cell):
    rows = v.shape[0] // 8
    total = None
    for flip in (0, 1):
        for s in range(4):
            owner = (core ^ flip) * 4 + ((cell + s) & 3)
            part = lax.dynamic_slice_in_dim(v, owner * rows, rows, axis=0)
            part = part if (flip, s) == (0, 0) else within(part, flip, s)
            total = part if total is None else total + part
    return total


def put_kernel(cell_ref, *refs):
    out_ref = refs[-1]
    rows = refs[0].shape[0]
    for s, ref in enumerate(refs[:-1]):
        place = ((cell_ref[0] - s) & 3) * rows
        out_ref[pl.ds(pl.multiple_of(place, rows), rows), :] = ref[...]


def join_kernel(core_ref, mine_ref, other_ref, out_ref):
    rows = mine_ref.shape[0]
    for ref, core in ((mine_ref, core_ref[0]), (other_ref, 1 - core_ref[0])):
        out_ref[pl.ds(pl.multiple_of(core * rows, rows), rows), :] = ref[...].astype(
            jnp.float32
        )


def gather_sum(parts, core, cell):
    rows, features = parts[0].shape
    mine = pl.pallas_call(
        put_kernel,
        in_specs=[SMEM] + [VMEM] * 4,
        out_specs=VMEM,
        out_shape=jax.ShapeDtypeStruct((4 * rows, features), parts[0].dtype),
        compiler_params=params(),
        name="put_parts",
    )(cell[None], *parts)
    return pl.pallas_call(
        join_kernel,
        in_specs=[SMEM] + [VMEM] * 2,
        out_specs=VMEM,
        out_shape=jax.ShapeDtypeStruct((8 * rows, features), jnp.float32),
        compiler_params=params(),
        name="join_halves",
    )(core[None], mine, within(mine, 1, 0))


def on_device(inputs, weight, band_vals, far_rows, far_send, far_count, far_vals, grad_out):
    x = inputs[0]
    band = band_vals[0]
    cap = far_send.shape[-1]
    send_index = far_send.reshape(-1)
    target_index = far_rows.reshape(-1)
    count = far_count.reshape(-1)
    vals = far_vals.reshape(-1, BLK, BLK)
    core = lax.axis_index("genome") & 1
    cell = lax.axis_index("cell")

    arrived = exchange(gather_blocks(x, far_send[0, 0].T, far_count[0]))
    low, high = to_neighbours(*rim_terms(x, band))
    band_part = band_sum(x, band)
    output, grads, y, terms = middle(
        cap, target_index, arrived, vals, band_part, low, high, weight, grad_out[0]
    )

    so_far = exchange(terms)
    rims = rim_terms(grads, band)
    rims, y = lax.optimization_barrier((rims, y))
    low, high = to_neighbours(*rims)
    part = scatter_sum(dot_ta(y, grads), core, cell)
    terms = back_terms(1, cap, target_index, grads, vals)
    part, terms = lax.optimization_barrier((part, terms))
    sent = part.astype(jnp.bfloat16)
    part = part + sum(shift(sent, "x", s).astype(jnp.float32) for s in (1, 2, 3))
    terms, so_far, part, grads = lax.optimization_barrier((terms, so_far, part, grads))

    came_back = exchange(terms)
    so_far = sum_back(0, cap, send_index, count, so_far, band_sum(grads, band), low, high)
    sent = part.astype(jnp.bfloat16)
    part = part + sum(shift(sent, "y", s).astype(jnp.float32) for s in (1, 2, 3))
    part, low, high = lax.optimization_barrier((part, low, high))
    sent = part.astype(jnp.bfloat16)
    grad_weight = gather_sum([sent] + [within(sent, 0, s) for s in (1, 2, 3)], core, cell)
    came_back, so_far, grad_weight = lax.optimization_barrier((came_back, so_far, grad_weight))
    grad_in = tail(1, cap, send_index, count, came_back, so_far, weight.T)
    return (output[None], grad_in[None], grad_weight)


def solution(mesh):
    return jax.shard_map(
        on_device,
        mesh=mesh,
        in_specs=(
            P("cell", "genome", None),
            P(),
            P("cell", "genome", None, None, None),
            P("cell", "genome", None, None),
            P("cell", "genome", None, None),
            P("cell", "genome", None),
            P("cell", "genome", None, None, None, None),
            P("cell", "genome", None),
        ),
        out_specs=(P("cell", "genome", None), P("cell", "genome", None), P()),
        check_vma=False,
    )
```
